32 devices in a mesh: dp: 8 (over z, x), cond: 4 (over y, core).
Axes of the slice: x: 2, y: 2, z: 4, core: 2. Of those that a mesh axis runs over, the one named last changes fastest.
Arguments:
- actions: float32 [4096, 256], P('dp'), may hold values from -6 to 6
- memory: bfloat16 [256, 800, 256], P('dp', 'cond'), may hold values from -6 to 6
- patch_flags: int32 [256, 4], P('dp', 'cond'), may hold values from 49 to 196, as said below
- memory_mask: int32 [256, 800], P('dp', 'cond'), may hold values 0 or 1
- cotangent: float32 [4096, 256], P('dp'), may hold values from -6 to 6
- row_weights: float32 [256, 2560], replicated
- memory_weights: float32 [256, 512], replicated, may hold values from -0.375 to 0.375
- down_weight: float32 [1024, 256], replicated, may hold values from -0.1875 to 0.1875
- vectors: float32 [11, 256], replicated
- row_momentum: float32 [256, 2560], replicated, may hold values from -0.25 to 0.25
- memory_momentum: float32 [256, 512], replicated, may hold values from -0.25 to 0.25
- down_momentum: float32 [1024, 256], replicated, may hold values from -0.25 to 0.25
- vector_momentum: float32 [11, 256], replicated, may hold values from -0.25 to 0.25
- row_average: float32 [256, 2560], replicated
- memory_average: float32 [256, 512], replicated, may hold values from -0.375 to 0.375
- down_average: float32 [1024, 256], replicated, may hold values from -0.1875 to 0.1875
- vector_average: float32 [11, 256], replicated
Outputs:
- output: float32 [4096, 256], P('dp')
- grad_actions: float32 [4096, 256], P('dp')
- grad_memory: float32 [256, 800, 256], P('dp', 'cond')
- row_momentum_new: float32 [256, 2560], replicated
- row_weights_new: float32 [256, 2560], replicated
- row_average_new: float32 [256, 2560], replicated
- memory_momentum_new: float32 [256, 512], replicated
- memory_weights_new: float32 [256, 512], replicated
- memory_average_new: float32 [256, 512], replicated
- down_momentum_new: float32 [1024, 256], replicated
- down_weight_new: float32 [1024, 256], replicated
- down_average_new: float32 [1024, 256], replicated
- vector_momentum_new: float32 [11, 256], replicated
- vectors_new: float32 [11, 256], replicated
- vector_average_new: float32 [11, 256], replicated
The draws below stay inside these ranges and needn't reach their ends.
Inputs may be any that keep to these rules, and one draw needn't show every extreme that they name: `patch_flags`: every entry is 49 or 196.
All inputs are finite; a program needn't handle non-finite values. No bound on the sum of `memory_mask` on one device may be relied on, other than what follows from the above.
Results may differ from the reference program's by a relative error of at most 0.02.
Values may be sent and summed in bfloat16 or wider, within the bound.
A program may use at most 128 MiB of HBM per device.

```python
import jax
import jax.numpy as jnp
from jax import lax

D = 256
HEADS = 4
FF = 1024
H = 16
PATCHES = 196
FEW = 49
STEP = 10
CAMERAS = 4
SLOTS = 200
MEM = 800
SAMPLES = 256
TOKENS = 4096
VEC_ROWS = 11


def row_law(key):
    columns = jnp.arange(6 * D + FF)
    factor = jnp.where(columns < 3 * D, 1.0, jnp.where(columns < 4 * D, 2.5, jnp.where(columns < 5 * D, 1.0, jnp.where(columns < 6 * D, 12.0, 1.0))))
    values = jax.random.normal(key, (D, 6 * D + FF), jnp.float32)
    return values * factor[None, :] * D ** (-0.5)


def vector_law(key):
    row_index = jnp.arange(VEC_ROWS)[:, None]
    gain_key, shift_key = jax.random.split(key)
    gain_draw = jax.random.uniform(gain_key, (VEC_ROWS, D), jnp.float32, 0.5, 1.5)
    shifts = 0.3 * jax.random.normal(shift_key, (VEC_ROWS, D), jnp.float32)
    is_gain = (row_index < 6) & (row_index % 2 == 0)
    return jnp.where(is_gain, gain_draw, shifts)


def draw_row_weights(key, part):
    key = jax.random.fold_in(key, 11)
    return row_law(key)


def draw_row_average(key, part):
    key = jax.random.fold_in(key, 12)
    return row_law(key)


def draw_vectors(key, part):
    key = jax.random.fold_in(key, 13)
    return vector_law(key)


def draw_vector_average(key, part):
    key = jax.random.fold_in(key, 14)
    return vector_law(key)


def draw_patch_flags(key, part):
    key = jax.random.fold_in(key, 21)
    coin_flips = jax.random.randint(key, (SAMPLES, CAMERAS), 0, 2)
    flags = jnp.where(coin_flips == 1, PATCHES, FEW).astype(jnp.int32)
    return flags.at[0, 0].set(PATCHES).at[0, 1].set(FEW)


def place_ends(values, stream_key, least, largest):
    longest = values.shape.index(max(values.shape))
    spots = []
    for shift in (0, 1):
        where = [jax.random.randint(jax.random.fold_in(stream_key, axis), (), 0, length) for axis, length in enumerate(values.shape)]
        where[longest] = (where[longest] + shift) % values.shape[longest]
        spots.append(tuple(where))
    return values.at[spots[0]].set(least).at[spots[1]].set(largest)


def shard_levels(stream_key, shape, pieces, low, largest):
    level = 1.0
    for axis_at, blocks in pieces:
        steps = jax.random.uniform(jax.random.fold_in(jax.random.fold_in(stream_key, 6), axis_at), (blocks,), jnp.float32, low / len(pieces), largest / len(pieces))
        level = level * jnp.repeat(jnp.exp(steps), shape[axis_at] // blocks).reshape((-1,) + (1,) * (len(shape) - 1 - axis_at))
    return level


def noise(stream_key, dims, scale, limit, shards=(), kind=jnp.bfloat16):
    array = scale * jax.random.normal(stream_key, dims, jnp.float32)
    if shards:
        array = array * shard_levels(stream_key, dims, shards, -0.22, 0.18)
    return jnp.clip(array, -limit, limit).astype(kind)


def setup_inputs(seed: int = 0) -> dict:
    key_of = jax.random.split(jax.random.key(seed), 18)
    return {
        "actions": noise(key_of[0], (TOKENS, D), 1.0, 6.0, ((0, 8),), jnp.float32),
        "memory": noise(key_of[1], (SAMPLES, MEM, D), 1.0, 6.0, ((0, 8), (1, 4))),
        "patch_flags": draw_patch_flags(jax.random.fold_in(key_of[17], 71), 0),
        "memory_mask": place_ends((jax.random.randint(key_of[3], (SAMPLES, MEM), 0, 8) < 7).astype(jnp.int32), jax.random.fold_in(key_of[3], 1), 0, 1),
        "cotangent": noise(key_of[4], (TOKENS, D), 1.0, 6.0, ((0, 8),), jnp.float32),
        "row_weights": draw_row_weights(jax.random.fold_in(key_of[17], 71), 0),
        "memory_weights": noise(key_of[6], (D, 2 * D), D ** -0.5, 0.375, (), jnp.float32),
        "down_weight": noise(key_of[7], (FF, D), FF ** -0.5, 0.1875, (), jnp.float32),
        "vectors": draw_vectors(jax.random.fold_in(key_of[17], 71), 0),
        "row_momentum": noise(key_of[9], (D, 6 * D + FF), (TOKENS ** -0.5), 0.25, (), jnp.float32),
        "memory_momentum": noise(key_of[10], (D, 2 * D), (TOKENS ** -0.5), 0.25, (), jnp.float32),
        "down_momentum": noise(key_of[11], (FF, D), (TOKENS ** -0.5), 0.25, (), jnp.float32),
        "vector_momentum": noise(key_of[12], (VEC_ROWS, D), (TOKENS ** -0.5), 0.25, (), jnp.float32),
        "row_average": draw_row_average(jax.random.fold_in(key_of[17], 71), 0),
        "memory_average": noise(key_of[14], (D, 2 * D), D ** -0.5, 0.375, (), jnp.float32),
        "down_average": noise(key_of[15], (FF, D), FF ** -0.5, 0.1875, (), jnp.float32),
        "vector_average": draw_vector_average(jax.random.fold_in(key_of[17], 71), 0),
    }


@jax.custom_vjp
def low(v):
    return lax.optimization_barrier(v.astype(jnp.bfloat16)).astype(jnp.float32)

@jax.custom_vjp
def low_back(v):
    return v

def low_keep(v):
    return (low(v), None)

def low_pass(kept, grad):
    return (grad,)

def back_keep(v):
    return (v, None)

def back_low(kept, grad):
    return (low(grad),)
low.defvjp(low_keep, low_pass)
low_back.defvjp(back_keep, back_low)
precise = lax.Precision.HIGHEST
inertia = 0.9
step_rate = 1.0

def round_both(values):
    return low(low_back(values))

def normed(values, norm_gain, norm_shift):
    centered = values - lax.optimization_barrier(jnp.mean(values, axis=-1, keepdims=True))
    spread = lax.optimization_barrier(jnp.mean(centered * centered, axis=-1, keepdims=True))
    return centered * lax.rsqrt(spread + 1e-05) * norm_gain + norm_shift

def softmax_rows(scores):
    shifted = jnp.exp(scores - lax.optimization_barrier(jnp.max(scores, axis=-1, keepdims=True)))
    return shifted / lax.optimization_barrier(jnp.sum(shifted, axis=-1, keepdims=True))

def decoder_layer(actions, memory, row_weights, memory_weights, down_weight, vectors, usable):
    samples = actions.shape[0] // H
    head_size = D // HEADS
    factor = head_size ** (-0.5)
    halves = low(row_weights)
    w_qkv = halves[:, :3 * D]
    w_self_out = halves[:, 3 * D:4 * D]
    w_cross_query = halves[:, 4 * D:5 * D]
    w_cross_out = halves[:, 5 * D:6 * D]
    w_up = halves[:, 6 * D:]
    w_pairs = low(memory_weights)
    w_down = low(down_weight)
    first_norm = low(normed(actions, vectors[0], vectors[1]))
    qkv = round_both(jnp.dot(first_norm, w_qkv, precision=precise)).reshape(samples, H, 3, HEADS, head_size)
    queries = qkv[:, :, 0]
    key_rows = qkv[:, :, 1]
    values = qkv[:, :, 2]
    causal = jnp.arange(H)[:, None] >= jnp.arange(H)[None, :]
    raw_scores = jnp.einsum('sihd,sjhd->shij', queries, key_rows, precision=precise) * factor
    scores = low_back(jnp.where(causal, raw_scores, -1e+30))
    self_probs = low(softmax_rows(scores))
    self_mix = round_both(jnp.einsum('shij,sjhd->sihd', self_probs, values, precision=precise)).reshape(samples * H, D)
    after_self = actions + low_back(jnp.dot(self_mix, w_self_out, precision=precise))
    second = low(normed(after_self, vectors[2], vectors[3]))
    cross_queries = round_both(jnp.dot(second, w_cross_query, precision=precise)).reshape(samples, H, HEADS, head_size)
    key_value = round_both(jnp.einsum('smd,de->sme', memory, w_pairs, precision=precise)).reshape(samples, CAMERAS, SLOTS, 2, HEADS, head_size)
    query_copies = low_back(jnp.broadcast_to(cross_queries[None], (CAMERAS, samples, H, HEADS, head_size)))
    raw_cross = jnp.einsum('csihd,scjhd->shicj', query_copies, key_value[:, :, :, 0], precision=precise).reshape(samples, HEADS, H, MEM) * factor
    cross_scores = low_back(jnp.where(usable[:, None, None, :], raw_cross, -1e+30))
    cross_probs = low(softmax_rows(cross_scores)).reshape(samples, HEADS, H, CAMERAS, SLOTS)
    partials = low(jnp.einsum('shicj,scjhd->csihd', cross_probs, key_value[:, :, :, 1], precision=precise))
    cross_mix = round_both(lax.optimization_barrier(jnp.sum(partials, axis=0))).reshape(samples * H, D)
    after_cross = after_self + low_back(jnp.dot(cross_mix, w_cross_out, precision=precise))
    third_norm = low(normed(after_cross, vectors[4], vectors[5]))
    bias_up = vectors[6:6 + FF // D].reshape(FF)
    pre_act = low_back(jnp.dot(third_norm, w_up, precision=precise) + bias_up)
    activated = low(jax.nn.gelu(pre_act, approximate=False))
    return after_cross + low_back(jnp.dot(activated, w_down, precision=precise) + vectors[6 + FF // D])

def update(weight, gradient, moment, average, token_count):
    average_rate = 1.0 - (1.0 + STEP) ** (-0.75)
    scaled = gradient / token_count
    moment_new = inertia * moment + scaled
    weight_new = weight - step_rate * (scaled + inertia * moment_new)
    average_new = average_rate * average + (1.0 - average_rate) * weight_new
    return (moment_new, weight_new, average_new)

def reference(actions, memory, patch_flags, memory_mask, cotangent, row_weights, memory_weights, down_weight, vectors, row_momentum, memory_momentum, down_momentum, vector_momentum, row_average, memory_average, down_average, vector_average):
    slot_index = jnp.arange(MEM) % SLOTS
    block_index = jnp.arange(MEM) // SLOTS
    counts = patch_flags[:, block_index]
    usable = (slot_index[None, :] < counts) & (memory_mask == 1) | ((block_index == 0) & (slot_index == PATCHES))[None, :]
    memory_full = memory.astype(jnp.float32)

    def forward(act_in, mem_in, row_in, pair_in, down_in, vec_in):
        return decoder_layer(act_in, mem_in, row_in, pair_in, down_in, vec_in, usable)
    output, pull = jax.vjp(forward, actions, memory_full, row_weights, memory_weights, down_weight, vectors)
    grad_actions, grad_memory, grad_rows, grad_pairs, grad_down, grad_vectors = pull(cotangent)
    token_count = float(actions.shape[0])
    row_new = update(row_weights, grad_rows, row_momentum, row_average, token_count)
    pair_new = update(memory_weights, grad_pairs, memory_momentum, memory_average, token_count)
    down_new = update(down_weight, grad_down, down_momentum, down_average, token_count)
    vector_new = update(vectors, grad_vectors, vector_momentum, vector_average, token_count)
    return (output, grad_actions, grad_memory, row_new[0], row_new[1], row_new[2], pair_new[0], pair_new[1], pair_new[2], down_new[0], down_new[1], down_new[2], vector_new[0], vector_new[1], vector_new[2])
```

```python
import functools
import math

import jax
import jax.numpy as jnp
from jax import lax
from jax.experimental import pallas as pl
from jax.experimental.pallas import tpu as pltpu
from jax.sharding import PartitionSpec as P

HEADS = 4
H = 16
PATCHES = 196
STEP = 10
INERTIA = 0.9
STEP_RATE = 1.0
LOWEST = -1e30
NB = 2
MESH = pl.DeviceIdType.MESH
MIB = 2**20
BF = jnp.bfloat16
F32 = jnp.float32


def half(values):
    return values.astype(BF)


def wide(values):
    return values.astype(F32)


def nn(a, b):
    return jnp.dot(a, b, preferred_element_type=F32)


def nt(a, b):
    return lax.dot_general(a, b, (((1,), (1,)), ((), ())), preferred_element_type=F32)


def tn(a, b):
    return lax.dot_general(a, b, (((0,), (0,)), ((), ())), preferred_element_type=F32)


def unit_rows(values):
    centered = values - jnp.mean(values, axis=-1, keepdims=True)
    rate = lax.rsqrt(jnp.mean(centered * centered, axis=-1, keepdims=True) + 1e-05)
    return centered * rate, rate


def unit_back(grad, unit, rate):
    return rate * (
        grad
        - jnp.mean(grad, axis=-1, keepdims=True)
        - unit * jnp.mean(grad * unit, axis=-1, keepdims=True)
    )


def column_sum(values):
    return jnp.sum(values, axis=0, keepdims=True)


def head_columns(table, first):
    rows = table.shape[0]
    low_lane = lax.broadcasted_iota(jnp.int32, (rows, 128), 1) < 64
    cols = [table[:, first + h : first + h + 1] for h in range(HEADS)]
    return jnp.concatenate(
        [jnp.where(low_lane, cols[0], cols[1]), jnp.where(low_lane, cols[2], cols[3])], axis=1
    )


def head_reduce(values, kind):
    rows = values.shape[0]
    low_lane = lax.broadcasted_iota(jnp.int32, (rows, 128), 1) < 64
    fill = LOWEST if kind == "max" else 0.0
    cols = []
    for pair in range(2):
        part = values[:, pair * 128 : pair * 128 + 128]
        for keep_low in (True, False):
            picked = jnp.where(low_lane == keep_low, part, fill)
            if kind == "max":
                cols.append(jnp.max(picked, axis=1, keepdims=True))
            else:
                cols.append(jnp.sum(picked, axis=1, keepdims=True))
    return cols


def spread(cols):
    rows = cols[0].shape[0]
    low_lane = lax.broadcasted_iota(jnp.int32, (rows, 128), 1) < 64
    return jnp.concatenate(
        [jnp.where(low_lane, cols[0], cols[1]), jnp.where(low_lane, cols[2], cols[3])], axis=1
    )


def lanes_of(cols):
    rows = cols[0].shape[0]
    lane = lax.broadcasted_iota(jnp.int32, (rows, 128), 1)
    table = jnp.zeros((rows, 128), F32)
    for h, col in enumerate(cols):
        table = jnp.where(lane == h, col, table)
    return table


def pad_rows(values, rows):
    missing = rows - values.shape[0]
    if missing == 0:
        return values
    return jnp.concatenate([values, jnp.zeros((missing, values.shape[1]), values.dtype)], axis=0)


def self_weights(q, k, blocks, causal):
    k_blocks = jnp.concatenate([k] * HEADS, axis=0) * blocks
    scores = jnp.where(causal, nt(q, k_blocks) * 0.125, LOWEST)
    top = spread(head_reduce(scores, "max"))
    raised = jnp.where(causal, jnp.exp(scores - top), 0.0)
    total = spread(head_reduce(raised, "sum"))
    return raised / total, k_blocks


class Names:
    pass


def layer_kernel(names, sizes, *refs):
    r = Names()
    for name, ref in zip(names, refs, strict=True):
        setattr(r, name, ref)
    rows, samples, slots, n_cond, n_dp, width = sizes
    hidden = r.dw.shape[0]
    part_rows = rows // NB
    own = part_rows // n_cond
    part_samples = samples // NB
    c = lax.axis_index("cond")
    d = lax.axis_index("dp")

    def peer(k):
        return (d, lax.rem(c + k, n_cond))

    core_peer = (d, c + 1 - 2 * lax.rem(c, 2))
    chip_peer = (d, lax.rem(c + 2, n_cond))
    bit0 = lax.rem(c, 2)
    bit1 = c // 2

    def row(k):
        return (lax.rem(d + k, n_dp), c)

    barrier = pltpu.get_barrier_semaphore()
    for k in range(1, n_cond):
        pl.semaphore_signal(barrier, inc=1, device_id=peer(k), device_id_type=MESH)
    for k in range(1, n_dp):
        pl.semaphore_signal(barrier, inc=1, device_id=row(k), device_id_type=MESH)

    loads = {}

    def load(name, src, dst, at):
        copy = pltpu.make_async_copy(src, dst, r.load_sem.at[at])
        copy.start()
        loads[name] = copy

    load("act", r.act_h, r.act, 0)
    load("rw", r.rw_h, r.rw, 1)
    load("vec", r.vec_h, r.vec, 2)
    load("mw", r.mw_h, r.mw, 3)
    mem_parts = 4
    mem_rows = samples * slots // mem_parts
    for i in range(mem_parts):
        span = pl.ds(i * mem_rows, mem_rows)
        load(f"mem{i}", r.mem_h.at[span], r.mem.at[span], 8 + i)
    load("mask", r.mask_h, r.mask, 4)
    load("flag", r.flag_h, r.flag, 5)
    load("dw", r.dw_h, r.dw, 6)
    load("cot", r.cot_h, r.cot, 7)

    lane256 = lax.broadcasted_iota(jnp.int32, (256, 256), 1)
    row256 = lax.broadcasted_iota(jnp.int32, (256, 256), 0)
    r.blocks[...] = half(jnp.where(lane256 // 64 == row256 // 64, 1.0, 0.0))
    lane64 = lax.broadcasted_iota(jnp.int32, (64, 256), 1)
    row64 = lax.broadcasted_iota(jnp.int32, (64, 256), 0)
    r.heads[...] = jnp.where(lane64 // 64 == row64 // 16, 1.0, 0.0)
    r.heads_b[...] = half(r.heads[...])

    def causal_mask():
        key = lax.rem(lane64, 64)
        return (key // H == row64 // H) & (key <= row64)

    loads["act"].wait()
    loads["rw"].wait()
    loads["vec"].wait()

    @pl.loop(0, 4)
    def _(i):
        span = pl.ds(pl.multiple_of(i * 64, 64), 64)
        r.rwb[span, :] = half(r.rw[span, :])

    def vec(i):
        return r.vec[i : i + 1, :]

    w_qkv = lambda: r.rwb[:, : 3 * width]
    w_so = lambda: r.rwb[:, 3 * width : 4 * width]
    w_cq = lambda: r.rwb[:, 4 * width : 5 * width]
    w_co = lambda: r.rwb[:, 5 * width : 6 * width]
    w_up = lambda: r.rwb[:, 6 * width :]

    def self_forward(b):
        group = 128

        @pl.loop(0, part_rows // group)
        def _(g):
            span = pl.ds(pl.multiple_of(b * part_rows + g * group, group), group)
            x = r.act[span, :]
            unit, _ = unit_rows(x)
            a1 = half(unit * vec(0) + vec(1))
            r.a1[span, :] = a1
            qkv = half(nn(a1, w_qkv()))
            r.qkv[span, :] = qkv
            causal = causal_mask()
            blocks = r.blocks[...]
            mixed = []
            for s in range(group // 64):
                piece = qkv[s * 64 : s * 64 + 64, :]
                q, k, v = (piece[:, i * width : (i + 1) * width] for i in range(3))
                weights, _ = self_weights(q, k, blocks, causal)
                v_blocks = jnp.concatenate([v] * HEADS, axis=0) * blocks
                mixed.append(nn(half(weights), v_blocks))
            o1 = half(jnp.concatenate(mixed, axis=0))
            r.o1[span, :] = o1
            x1 = x + nn(o1, w_so())
            r.x1[span, :] = x1
            unit2, _ = unit_rows(x1)
            a2 = half(unit2 * vec(2) + vec(3))
            r.a2[span, :] = a2
            r.qs[span, :] = half(nn(a2, w_cq()) * 0.125)

    def pair_forward(b):
        batch = 4
        step = batch * slots

        @pl.loop(0, part_samples // batch)
        def _(g):
            first = b * part_samples + g * batch
            span = pl.ds(pl.multiple_of(first * slots, step), step)
            chunk = r.mem[span, :]
            for side in range(2):
                cols = slice(side * width, (side + 1) * width)
                kv = nn(chunk, r.mwb[:, cols])
                for s in range(batch):
                    r.kv[first + s, :, cols] = half(kv[s * slots : (s + 1) * slots, :])

    def usable_rows():
        position = lax.broadcasted_iota(jnp.int32, (samples, slots), 1)
        kept = (position < r.flag[...]) & (r.mask[...] == 1)
        time_token = (position == PATCHES) & (c == 0)
        r.use[...] = jnp.where(kept | time_token, 1.0, 0.0)

    def cross_forward(b):
        unroll = 2

        @pl.loop(0, part_samples // unroll)
        def _(g):
            for i in range(unroll):
                s = b * part_samples + g * unroll + i
                span = pl.ds(pl.multiple_of(s * H, H), H)
                q = jnp.concatenate([r.qs[span, :]] * HEADS, axis=0) * r.heads_b[...]
                usable = jnp.broadcast_to(r.use[pl.ds(s, 1), :], (64, slots)) > 0.5
                scores = jnp.where(usable, nt(q, r.kv[s, :, :width]), LOWEST)
                top = jnp.max(scores, axis=1, keepdims=True)
                raised = jnp.where(usable, jnp.exp(scores - top), 0.0)
                total = jnp.sum(raised, axis=1, keepdims=True)
                p = half(raised)
                r.p[s] = p
                mixed = nn(p, r.kv[s, :, width:]) * r.heads[...]
                r.o_out[span, :] = half(sum(mixed[h * H : h * H + H, :] for h in range(HEADS)))
                r.top[span, :] = lanes_of([top[h * H : h * H + H, :] for h in range(HEADS)])
                r.total[span, :] = lanes_of([total[h * H : h * H + H, :] for h in range(HEADS)])

    pending = []

    def send(src, dst, at, to):
        copy = pltpu.make_async_remote_copy(
            src_ref=src,
            dst_ref=dst,
            send_sem=r.ssem.at[at],
            recv_sem=r.rsem.at[at],
            device_id=to,
            device_id_type=MESH,
        )
        copy.start()
        pending.append(copy)
        return copy

    def own_span(b, owner):
        return pl.ds(pl.multiple_of(b * part_rows + owner * own, own), own)

    flights = {}

    def send_mixed(b):
        for k in range(n_cond):
            owner = lax.rem(c + k, n_cond)
            span = own_span(b, owner)
            stats = jnp.concatenate(
                [
                    pad_rows(r.top[span, :], 128).T[:8, :],
                    pad_rows(r.total[span, :], 128).T[:8, :],
                ],
                axis=0,
            )
            if k == 0:
                r.st_in[b, 0] = stats
                r.o_in[b, 0] = r.o_out[span, :]
            else:
                r.st_out[b, k] = stats
                at = (b * n_cond + k) * 2
                flights["o", b, k] = (
                    send(r.st_out.at[b, k], r.st_in.at[b, k], at, peer(k)),
                    send(r.o_out.at[span, :], r.o_in.at[b, k], at + 1, peer(k)),
                )

    def middle(b):
        for k in range(1, n_cond):
            for copy in flights["o", b, k]:
                copy.wait_recv()
        me = own_span(b, c)
        mine = pl.ds(b * own, own)
        tops = [r.st_in[b, k, :8, :] for k in range(n_cond)]
        top = functools.reduce(jnp.maximum, tops)
        raised = [jnp.exp(t - top) for t in tops]
        total = sum(w * r.st_in[b, k, 8:, :] for k, w in enumerate(raised))
        total = jnp.maximum(total, 0.5)
        shares = [w / total for w in raised]
        table = pad_rows(jnp.concatenate(shares, axis=0), 128).T[:own, :]
        spreads = [head_columns(table, 8 * k) for k in range(n_cond)]
        o2 = sum(spreads[k] * wide(r.o_in[b, k]) for k in range(n_cond))
        o2b = half(o2)
        r.o2[mine, :] = o2b
        x2 = r.x1[me, :] + nn(o2b, w_co())
        unit, rate = unit_rows(x2)
        a3 = half(unit * vec(4) + vec(5))
        r.a3[mine, :] = a3
        biases = hidden // width
        cot = r.cot[me, :]
        dz = half(cot)
        r.dz[mine, :] = dz
        out = x2 + vec(6 + biases)
        da3 = jnp.zeros((own, width), F32)
        for j in range(biases):
            cols = slice(6 * width + j * width, 6 * width + (j + 1) * width)
            here = slice(j * width, (j + 1) * width)
            u = nn(a3, r.rwb[:, cols]) + vec(6 + j)
            below = 0.5 + 0.5 * lax.erf(u * (2.0**-0.5))
            hb = half(u * below)
            r.hb[mine, here] = hb
            out = out + nn(hb, r.dwb[here, :])
            slope = below + u * (jnp.exp(-0.5 * u * u) * (1.0 / math.sqrt(2.0 * math.pi)))
            du = half(nt(dz, r.dwb[here, :]) * slope)
            r.du[mine, here] = du
            add_vec(b, 6 + j, column_sum(wide(du)))
            da3 = da3 + nt(du, r.rwb[:, cols])
        r.out16[me, :] = half(out)
        add_vec(b, 6 + biases, column_sum(wide(dz)))
        add_vec(b, 4, column_sum(da3 * unit))
        add_vec(b, 5, column_sum(da3))
        dx2 = cot + unit_back(da3 * vec(4), unit, rate)
        r.dx2[mine, :] = dx2
        dy = half(dx2)
        r.dy2[mine, :] = dy
        do2 = wide(half(nt(dy, w_co())))
        delta = lanes_of(head_reduce(do2 * wide(o2b), "sum"))
        delta = pad_rows(delta, 128).T[:8, :]
        for k in range(n_cond):
            grads = half(do2 * spreads[k])
            dots = delta * shares[k]
            if k == 0:
                r.do_in[me, :] = grads
                r.dl_in[b, 0] = dots
            else:
                r.do_out[b, k] = grads
                r.dl_out[b, k] = dots
                at = (NB * n_cond + b * n_cond + k) * 2
                to = peer(n_cond - k)
                flights["do", b, k] = (
                    send(r.dl_out.at[b, k], r.dl_in.at[b, k], at, to),
                    send(r.do_out.at[b, k], r.do_in.at[me, :], at + 1, to),
                )

    def add_vec(b, i, values):
        if b == 0:
            r.vg[i : i + 1, :] = values
        else:
            r.vg[i : i + 1, :] += values

    def cross_backward(b):
        for k in range(n_cond):
            owner = lax.rem(c + k, n_cond)
            if k:
                for copy in flights["do", b, k]:
                    copy.wait_recv()
            r.dl[own_span(b, owner), :] = pad_rows(r.dl_in[b, k], 128).T[:own, :]
        unroll = 2

        @pl.loop(0, part_samples // unroll)
        def _(g):
            pairs = []
            first = b * part_samples + g * unroll
            for i in range(unroll):
                s = first + i
                span = pl.ds(pl.multiple_of(s * H, H), H)
                heads_b = r.heads_b[...]
                q = jnp.concatenate([r.qs[span, :]] * HEADS, axis=0) * heads_b
                grads = jnp.concatenate([r.do_in[span, :]] * HEADS, axis=0) * heads_b
                dots = r.dl[span, :]
                dots = jnp.concatenate([dots[:, h : h + 1] for h in range(HEADS)], axis=0)
                p = r.p[s]
                ds = half(wide(p) * (nt(grads, r.kv[s, :, width:]) - dots))
                dq = nn(ds, r.kv[s, :, :width]) * r.heads[...]
                dq = sum(dq[h * H : h * H + H, :] for h in range(HEADS)) * 0.125
                r.dq_out[span, :] = half(dq)
                pairs.append(jnp.concatenate([tn(ds, q), tn(p, grads)], axis=1))
            span = pl.ds(pl.multiple_of(first * slots, unroll * slots), unroll * slots)
            r.dkv[span, :] = half(jnp.concatenate(pairs, axis=0))

    def send_query_grads(b):
        for k in range(1, n_cond):
            owner = lax.rem(c + k, n_cond)
            at = 4 * NB * n_cond + b * n_cond + k
            flights["dq", b, k] = send(
                r.dq_out.at[own_span(b, owner), :], r.dq_in.at[b, k], at, peer(k)
            )

    def self_backward(b):
        me = own_span(b, c)
        mine = pl.ds(b * own, own)
        total = wide(r.dq_out[me, :])
        for k in range(1, n_cond):
            flights["dq", b, k].wait_recv()
            total = total + wide(r.dq_in[b, k])
        dqc = half(total)
        r.dqc[mine, :] = dqc
        da2 = nt(dqc, w_cq())
        unit2, rate2 = unit_rows(r.x1[me, :])
        add_vec(b, 2, column_sum(da2 * unit2))
        add_vec(b, 3, column_sum(da2))
        dx1 = r.dx2[mine, :] + unit_back(da2 * vec(2), unit2, rate2)
        dy1 = half(dx1)
        r.dy1[mine, :] = dy1
        do1 = half(nt(dy1, w_so()))
        causal = causal_mask()
        blocks = r.blocks[...]
        pieces = []
        for s in range(own // 64):
            span = pl.ds(pl.multiple_of(b * part_rows + c * own + s * 64, 64), 64)
            q, k, v = (r.qkv[span, i * width : (i + 1) * width] for i in range(3))
            grads = do1[s * 64 : s * 64 + 64, :]
            weights, k_blocks = self_weights(q, k, blocks, causal)
            v_blocks = jnp.concatenate([v] * HEADS, axis=0) * blocks
            dv = tn(half(weights), grads) * wide(blocks)
            dp = nt(grads, v_blocks)
            dots = spread(head_reduce(weights * dp, "sum"))
            ds = half(weights * (dp - dots))
            dq = nn(ds, k_blocks) * 0.125
            dk = tn(ds, q) * wide(blocks)
            dk = sum(dk[h * 64 : h * 64 + 64, :] for h in range(HEADS)) * 0.125
            dv = sum(dv[h * 64 : h * 64 + 64, :] for h in range(HEADS))
            pieces.append(half(jnp.concatenate([dq, dk, dv], axis=1)))
        dqkv = jnp.concatenate(pieces, axis=0)
        r.dqkv[mine, :] = dqkv
        da1 = nt(dqkv, w_qkv())
        unit1, rate1 = unit_rows(r.act[me, :])
        add_vec(b, 0, column_sum(da1 * unit1))
        add_vec(b, 1, column_sum(da1))
        r.ga16[me, :] = half(dx1 + unit_back(da1 * vec(0), unit1, rate1))

    layout = {"ffn": (0, 2 * hidden), "row": (2 * hidden, 6 * width)}
    layout["pair"] = (2 * hidden + 6 * width, 2 * width)
    set_at = {name: 5 * NB * n_cond + 8 + 6 * i for i, name in enumerate(layout)}

    def owned(ref, dyn):
        return jnp.concatenate([ref[own_span(b, c), :] for b in range(NB)], axis=0)

    def ffn_grads():
        for j in range(hidden // width):
            here = slice(j * width, (j + 1) * width)
            r.g[j * width : (j + 1) * width, :] = half(tn(r.a3[...], r.du[:, here]))
            at = hidden + j * width
            r.g[at : at + width, :] = half(tn(r.hb[:, here], r.dz[...]))

    def put_row(j, values):
        first = layout["row"][0] + j * width
        r.g[first : first + width, :] = half(values)

    def row_grads():
        put_row(0, tn(r.o2[...], r.dy2[...]))
        put_row(1, tn(owned(r.a2, c), r.dqc[...]))
        put_row(2, tn(owned(r.o1, c), r.dy1[...]))
        a1 = owned(r.a1, c)
        for j in range(3):
            put_row(3 + j, tn(a1, r.dqkv[:, j * width : (j + 1) * width]))

    def pair_grads():
        step = 2 * slots
        r.gw[...] = jnp.zeros_like(r.gw)

        @pl.loop(0, samples // 2)
        def _(g):
            span = pl.ds(pl.multiple_of(g * step, step), step)
            r.gw[...] += tn(r.mem[span, :], r.dkv[span, :])

        first = layout["pair"][0]
        for side in range(2):
            r.g[first + side * width : first + (side + 1) * width, :] = half(
                r.gw[:, side * width : (side + 1) * width]
            )

    def set_sizes(name):
        first, count = layout[name]
        quarter = count // 4
        piece = max(16, quarter // n_dp)
        return first, count, count // 2, quarter, piece, quarter // piece

    def at_rows(start, count):
        return pl.ds(pl.multiple_of(start, 16), count)

    def reduce_core(name):
        first, count, two, four, piece, owners = set_sizes(name)
        flights[name, 0] = send(
            r.g.at[at_rows(first + (1 - bit0) * two, two), :],
            r.rc.at[at_rows(first // 2, two), :],
            set_at[name],
            core_peer,
        )

    def reduce_chip(name):
        first, count, two, four, piece, owners = set_sizes(name)
        flights[name, 0].wait_recv()
        base = first // 2
        for q in range(2):
            span = pl.ds(base + q * four, four)
            got = wide(r.rc[span, :]) + wide(
                r.g[at_rows(first + bit0 * two + q * four, four), :]
            )
            r.rc[span, :] = half(got)
        flights[name, 1] = send(
            r.rc.at[at_rows(base + (1 - bit1) * four, four), :],
            r.ry.at[pl.ds(first // 4, four), :],
            set_at[name] + 1,
            chip_peer,
        )

    def wait_bytes(name, stage, ref, count, which):
        view = ref.at[pl.ds(0, count), :]
        copy = pltpu.make_async_remote_copy(
            src_ref=view,
            dst_ref=view,
            send_sem=r.ssem.at[set_at[name] + stage],
            recv_sem=r.rsem.at[set_at[name] + stage],
            device_id=core_peer,
            device_id_type=MESH,
        )
        if which == "recv":
            copy.wait_recv()
        else:
            copy.wait_send()

    def start(src, dst, at, to):
        pltpu.make_async_remote_copy(
            src_ref=src,
            dst_ref=dst,
            send_sem=r.ssem.at[at],
            recv_sem=r.rsem.at[at],
            device_id=to,
            device_id_type=MESH,
        ).start()

    def guard(full, cond, body):
        if full:
            body()
        else:
            pl.when(cond)(body)

    def reduce_rows(name):
        first, count, two, four, piece, owners = set_sizes(name)
        flights[name, 1].wait_recv()
        base = first // 4
        mine = wide(r.rc[at_rows(first // 2 + bit1 * four, four), :])
        span = pl.ds(base, four)
        r.ry[span, :] = half(mine + wide(r.ry[span, :]))
        for k in range(1, n_dp):
            to = lax.rem(d + k, n_dp)

            def go(k=k, to=to):
                start(
                    r.ry.at[at_rows(base + to * piece, piece), :],
                    r_rd(name).at[pl.ds(k * piece, piece), :],
                    set_at[name] + 2,
                    row(k),
                )

            guard(owners == n_dp, to < owners, go)

    def r_rd(name):
        return getattr(r, "rd_" + name)

    def quarter_at(name):
        first, count, two, four, piece, owners = set_sizes(name)
        return first + bit0 * two + bit1 * four

    def gather_rows(name):
        first, count, two, four, piece, owners = set_sizes(name)
        base = first // 4

        def finish():
            wait_bytes(name, 2, r_rd(name), (n_dp - 1) * piece, "recv")
            total = wide(r.ry[at_rows(base + d * piece, piece), :])
            for k in range(1, n_dp):
                total = total + wide(r_rd(name)[k * piece : (k + 1) * piece, :])
            here = at_rows(quarter_at(name) + d * piece, piece)
            r.tot[here, :] = half(total)
            for k in range(1, n_dp):
                start(r.tot.at[here, :], r.tot.at[here, :], set_at[name] + 3, row(k))

        guard(owners == n_dp, d < owners, finish)

    def gather_chip(name):
        first, count, two, four, piece, owners = set_sizes(name)
        if owners == n_dp:
            wait_bytes(name, 3, r.tot, (n_dp - 1) * piece, "recv")
        else:
            pl.when(d < owners)(
                lambda: wait_bytes(name, 3, r.tot, (owners - 1) * piece, "recv")
            )
            pl.when(d >= owners)(lambda: wait_bytes(name, 3, r.tot, owners * piece, "recv"))
        span = at_rows(quarter_at(name), four)
        flights[name, 4] = send(
            r.tot.at[span, :], r.tot.at[span, :], set_at[name] + 4, chip_peer
        )

    def gather_core(name):
        first, count, two, four, piece, owners = set_sizes(name)
        flights[name, 4].wait_recv()
        span = at_rows(first + bit0 * two, two)
        flights[name, 5] = send(
            r.tot.at[span, :], r.tot.at[span, :], set_at[name] + 5, core_peer
        )

    def end_set(name):
        first, count, two, four, piece, owners = set_sizes(name)
        flights[name, 5].wait_recv()
        if owners == n_dp:
            wait_bytes(name, 2, r.ry, (n_dp - 1) * piece, "send")
            wait_bytes(name, 3, r.tot, (n_dp - 1) * piece, "send")
        else:
            pl.when(d < owners)(
                lambda: wait_bytes(name, 2, r.ry, (owners - 1) * piece, "send")
            )
            pl.when(d >= owners)(lambda: wait_bytes(name, 2, r.ry, owners * piece, "send"))
            pl.when(d < owners)(lambda: wait_bytes(name, 3, r.tot, (n_dp - 1) * piece, "send"))

    vec_at = 5 * NB * n_cond + 8 + 6 * len(layout)

    def small_cond():
        r.vc_in[pl.ds(c, 1)] = r.vg[...][None]
        for k in range(1, n_cond):
            flights["vc", k] = send(r.vg, r.vc_in.at[c], vec_at + k - 1, peer(k))

    def small_rows():
        for k in range(1, n_cond):
            flights["vc", k].wait_recv()
        r.vd_in[pl.ds(d, 1)] = sum(r.vc_in[k] for k in range(n_cond))[None]
        for k in range(1, n_dp):
            start(r.vd_in.at[d], r.vd_in.at[d], vec_at + 3, row(k))

    def small_wait(which):
        view = r.vd_in.at[pl.ds(0, n_dp - 1)]
        copy = pltpu.make_async_remote_copy(
            src_ref=view,
            dst_ref=view,
            send_sem=r.ssem.at[vec_at + 3],
            recv_sem=r.rsem.at[vec_at + 3],
            device_id=core_peer,
            device_id_type=MESH,
        )
        copy.wait_recv() if which == "recv" else copy.wait_send()

    def small_end():
        small_wait("recv")
        total = r.vd_in[0]
        for k in range(1, n_dp):
            total = total + r.vd_in[k]
        r.vtot[...] = total
        small_wait("send")

    def share(name, ref, b):
        span = own_span(b, c)
        for k in range(1, n_cond):
            flights[name, b, k] = send(
                ref.at[span, :], ref.at[span, :], vec_at + 4 + len(shared), peer(k)
            )
            shared.append((name, b, k))

    shared = []

    r.vg[11:16, :] = jnp.zeros((5, width), F32)
    self_forward(0)
    loads["mw"].wait()
    r.mwb[...] = half(r.mw[...])
    loads["mask"].wait()
    loads["flag"].wait()
    usable_rows()
    for i in range(mem_parts // NB):
        loads[f"mem{i}"].wait()
    pair_forward(0)
    cross_forward(0)
    pl.semaphore_wait(barrier, n_cond - 1 + n_dp - 1)
    send_mixed(0)
    loads["dw"].wait()
    r.dwb[...] = half(r.dw[...])
    loads["cot"].wait()
    for b in range(1, NB):
        self_forward(b)
        for i in range(b * mem_parts // NB, (b + 1) * mem_parts // NB):
            loads[f"mem{i}"].wait()
        pair_forward(b)
        cross_forward(b)
        send_mixed(b)
    for b in range(NB):
        middle(b)
    ffn_grads()
    reduce_core("ffn")
    for b in range(NB):
        cross_backward(b)
        send_query_grads(b)
        if b == 0:
            reduce_chip("ffn")
        if b == NB - 1:
            reduce_rows("ffn")
    pair_grads()
    reduce_core("pair")
    for b in range(NB):
        self_backward(b)
        if b == 0:
            reduce_chip("pair")
            gather_rows("ffn")
    small_cond()
    row_grads()
    reduce_core("row")
    reduce_rows("pair")
    gather_chip("ffn")
    reduce_chip("row")
    small_rows()
    gather_rows("pair")
    reduce_rows("row")
    for b in range(NB):
        share("out16", r.out16, b)
        share("ga16", r.ga16, b)
    gather_core("ffn")
    gather_chip("pair")
    gather_rows("row")
    gather_core("pair")
    gather_chip("row")
    gather_core("row")
    small_end()
    for key in shared:
        flights[key].wait_recv()
    for name in layout:
        end_set(name)
    for copy in pending:
        copy.wait_send()


def step_kernel(names, token_count, *refs):
    r = Names()
    for name, ref in zip(names, refs, strict=True):
        setattr(r, name, ref)
    width = r.w_p.shape[0]
    hidden = r.w_d.shape[0]
    keep = 1.0 - (1.0 + STEP) ** (-0.75)
    copies = []

    def store(src, dst):
        copy = pltpu.make_async_copy(src, dst, r.sem.at[len(copies)])
        copy.start()
        copies.append(copy)

    r.mwb[...] = half(r.w_p[...])
    total_rows = r.dkv.shape[0]
    chunks = 8
    step = total_rows // chunks
    for i in range(chunks):
        inner = 2
        small = step // inner

        @pl.loop(0, inner)
        def _(j, i=i):
            span = pl.ds(pl.multiple_of(i * step + j * small, 16), small)
            r.gm[span, :] = nt(r.dkv[span, :], r.mwb[...])

        span = pl.ds(i * step, step)
        store(r.gm.at[span, :], r.gm_h.at[span, :])
    r.out[...] = wide(r.out16[...])
    store(r.out, r.out_h)
    r.ga[...] = wide(r.ga16[...])
    store(r.ga, r.ga_h)

    def update(weight, grad, moment, average):
        scaled = grad / token_count
        moment_new = INERTIA * moment + scaled
        weight_new = weight - STEP_RATE * (scaled + INERTIA * moment_new)
        average_new = keep * average + (1.0 - keep) * weight_new
        return moment_new, weight_new, average_new

    def group(prefix, views):
        w, m, a = (getattr(r, kind + "_" + prefix) for kind in "wma")
        for rows, cols, grad in views:
            new = update(w[rows, cols], grad(), m[rows, cols], a[rows, cols])
            for kind, value in zip("mwa", new):
                getattr(r, prefix + kind)[rows, cols] = value
        for kind in "mwa":
            store(getattr(r, prefix + kind), getattr(r, prefix + kind + "_h"))

    every = slice(None)
    row_first = 2 * hidden
    pair_first = row_first + 6 * width
    order = {5: 0, 4: 1, 3: 2, 0: 3, 1: 4, 2: 5}

    def table(first):
        return lambda: wide(r.tot[first : first + width, :])

    group(
        "d",
        [
            (slice(j * width, (j + 1) * width), every, table(hidden + j * width))
            for j in range(hidden // width)
        ],
    )
    group(
        "r",
        [
            (every, slice(j * width, (j + 1) * width), table(row_first + order[j] * width))
            for j in range(6)
        ]
        + [
            (every, slice((6 + j) * width, (7 + j) * width), table(j * width))
            for j in range(hidden // width)
        ],
    )
    group(
        "p",
        [
            (every, slice(j * width, (j + 1) * width), table(pair_first + j * width))
            for j in range(2)
        ],
    )
    group("v", [(every, every, lambda: r.vtot[: r.w_v.shape[0], :])])
    for copy in copies:
        copy.wait()


def per_device(
    actions,
    memory,
    patch_flags,
    memory_mask,
    cotangent,
    row_weights,
    memory_weights,
    down_weight,
    vectors,
    row_momentum,
    memory_momentum,
    down_momentum,
    vector_momentum,
    row_average,
    memory_average,
    down_average,
    vector_average,
):
    rows, width = actions.shape
    samples = rows // H
    slots = memory.shape[1]
    hidden = down_weight.shape[0]
    n_cond = lax.axis_size("cond")
    n_dp = lax.axis_size("dp")
    part_rows = rows // NB
    own = part_rows // n_cond
    total = 2 * hidden + 8 * width
    flat = samples * slots
    ins = {
        "act_h": actions,
        "mem_h": memory.reshape(flat, width),
        "mask_h": memory_mask,
        "flag_h": patch_flags,
        "cot_h": cotangent,
        "rw_h": row_weights,
        "mw_h": memory_weights,
        "dw_h": down_weight,
        "vec_h": vectors,
    }
    outs = {
        "tot": ((total, width), BF),
        "vtot": ((16, width), F32),
        "dkv": ((flat, 2 * width), BF),
        "out16": ((rows, width), BF),
        "ga16": ((rows, width), BF),
    }

    def pieces(count):
        return n_dp * max(16, count // 4 // n_dp)

    scratch = {
        "act": ((rows, width), F32),
        "rw": (row_weights.shape, F32),
        "vec": (vectors.shape, F32),
        "mw": (memory_weights.shape, F32),
        "mem": ((flat, width), BF),
        "mask": (memory_mask.shape, jnp.int32),
        "flag": (patch_flags.shape, jnp.int32),
        "dw": (down_weight.shape, F32),
        "cot": ((rows, width), F32),
        "rwb": (row_weights.shape, BF),
        "mwb": (memory_weights.shape, BF),
        "dwb": (down_weight.shape, BF),
        "blocks": ((256, 256), BF),
        "heads": ((64, 256), F32),
        "heads_b": ((64, 256), BF),
        "a1": ((rows, width), BF),
        "qkv": ((rows, 3 * width), BF),
        "o1": ((rows, width), BF),
        "x1": ((rows, width), F32),
        "a2": ((rows, width), BF),
        "qs": ((rows, width), BF),
        "kv": ((samples, slots, 2 * width), BF),
        "use": ((samples, slots), F32),
        "p": ((samples, 64, slots), BF),
        "o_out": ((rows, width), BF),
        "top": ((rows, 128), F32),
        "total": ((rows, 128), F32),
        "st_in": ((NB, n_cond, 16, 128), F32),
        "st_out": ((NB, n_cond, 16, 128), F32),
        "o_in": ((NB, n_cond, own, width), BF),
        "o2": ((NB * own, width), BF),
        "a3": ((NB * own, width), BF),
        "dz": ((NB * own, width), BF),
        "hb": ((NB * own, hidden), BF),
        "du": ((NB * own, hidden), BF),
        "dx2": ((NB * own, width), F32),
        "dy2": ((NB * own, width), BF),
        "dqc": ((NB * own, width), BF),
        "dy1": ((NB * own, width), BF),
        "dqkv": ((NB * own, 3 * width), BF),
        "do_in": ((rows, width), BF),
        "do_out": ((NB, n_cond, own, width), BF),
        "dl_in": ((NB, n_cond, 8, 128), F32),
        "dl_out": ((NB, n_cond, 8, 128), F32),
        "dl": ((rows, 128), F32),
        "dq_out": ((rows, width), BF),
        "dq_in": ((NB, n_cond, own, width), BF),
        "vg": ((16, width), F32),
        "vc_in": ((n_cond, 16, width), F32),
        "vd_in": ((n_dp, 16, width), F32),
        "g": ((total, width), BF),
        "gw": ((width, 2 * width), F32),
        "rc": ((total // 2, width), BF),
        "ry": ((total // 4, width), BF),
        "rd_ffn": ((pieces(2 * hidden), width), BF),
        "rd_row": ((pieces(6 * width), width), BF),
        "rd_pair": ((pieces(2 * width), width), BF),
    }
    sems = {
        "load_sem": pltpu.SemaphoreType.DMA((16,)),
        "ssem": pltpu.SemaphoreType.DMA((96,)),
        "rsem": pltpu.SemaphoreType.DMA((96,)),
    }
    whole = pl.BlockSpec(memory_space=pltpu.VMEM)
    far = pl.BlockSpec(memory_space=pl.ANY)
    names = list(ins) + list(outs) + list(scratch) + list(sems)
    sizes = (rows, samples, slots, n_cond, n_dp, width)
    tot, vtot, dkv, out16, ga16 = pl.pallas_call(
        functools.partial(layer_kernel, names, sizes),
        out_shape=[jax.ShapeDtypeStruct(*v) for v in outs.values()],
        in_specs=[far] * len(ins),
        out_specs=[whole] * len(outs),
        scratch_shapes=[pltpu.VMEM(*v) for v in scratch.values()] + list(sems.values()),
        compiler_params=pltpu.CompilerParams(
            collective_id=0, has_side_effects=True, vmem_limit_bytes=44 * MIB
        ),
        name="layer",
    )(*ins.values())

    ins2 = {
        "tot": tot,
        "vtot": vtot,
        "dkv": dkv,
        "out16": out16,
        "ga16": ga16,
        "w_r": row_weights,
        "w_p": memory_weights,
        "w_d": down_weight,
        "w_v": vectors,
        "m_r": row_momentum,
        "m_p": memory_momentum,
        "m_d": down_momentum,
        "m_v": vector_momentum,
        "a_r": row_average,
        "a_p": memory_average,
        "a_d": down_average,
        "a_v": vector_average,
    }
    outs2 = {
        "out": (rows, width),
        "ga": (rows, width),
        "gm": (flat, width),
    }
    for prefix, array in (("r", row_weights), ("p", memory_weights), ("d", down_weight), ("v", vectors)):
        for kind in "mwa":
            outs2[prefix + kind] = array.shape
    names2 = list(ins2) + [k + "_h" for k in outs2] + list(outs2) + ["mwb", "sem"]
    results = pl.pallas_call(
        functools.partial(step_kernel, names2, float(rows * n_dp)),
        out_shape=[jax.ShapeDtypeStruct(v, F32) for v in outs2.values()],
        in_specs=[whole] * len(ins2),
        out_specs=[far] * len(outs2),
        scratch_shapes=[pltpu.VMEM(v, F32) for v in outs2.values()]
        + [pltpu.VMEM(memory_weights.shape, BF), pltpu.SemaphoreType.DMA((32,))],
        compiler_params=pltpu.CompilerParams(vmem_limit_bytes=60 * MIB),
        name="step",
    )(*ins2.values())
    out, ga, gm = results[:3]
    return (out, ga, gm.reshape(samples, slots, width), *results[3:])


def solution(mesh):
    in_specs = (
        P("dp", None),
        P("dp", "cond", None),
        P("dp", "cond"),
        P("dp", "cond"),
        P("dp", None),
    ) + (P(),) * 12
    out_specs = (P("dp", None), P("dp", None), P("dp", "cond", None)) + (P(),) * 12
    return jax.shard_map(
        per_device, mesh=mesh, in_specs=in_specs, out_specs=out_specs, check_vma=False
    )
```

```python
import functools
import math

import jax
import jax.numpy as jnp
from jax import lax
from jax.experimental import pallas as pl
from jax.experimental.pallas import tpu as pltpu
from jax.sharding import PartitionSpec as P

HEADS = 4
H = 16
PATCHES = 196
STEP = 10
INERTIA = 0.9
STEP_RATE = 1.0
LOWEST = -1e30
NB = 2
MESH = pl.DeviceIdType.MESH
MIB = 2**20
BF = jnp.bfloat16
F32 = jnp.float32


def half(values):
    return values.astype(BF)


def wide(values):
    return values.astype(F32)


def nn(a, b):
    return jnp.dot(a, b, preferred_element_type=F32)


def nt(a, b):
    return lax.dot_general(a, b, (((1,), (1,)), ((), ())), preferred_element_type=F32)


def tn(a, b):
    return lax.dot_general(a, b, (((0,), (0,)), ((), ())), preferred_element_type=F32)


def unit_rows(values):
    centered = values - jnp.mean(values, axis=-1, keepdims=True)
    rate = lax.rsqrt(jnp.mean(centered * centered, axis=-1, keepdims=True) + 1e-05)
    return centered * rate, rate


def unit_back(grad, unit, rate):
    return rate * (
        grad
        - jnp.mean(grad, axis=-1, keepdims=True)
        - unit * jnp.mean(grad * unit, axis=-1, keepdims=True)
    )


def column_sum(values):
    return jnp.sum(values, axis=0, keepdims=True)


def head_columns(table, first):
    rows = table.shape[0]
    low_lane = lax.broadcasted_iota(jnp.int32, (rows, 128), 1) < 64
    cols = [table[:, first + h : first + h + 1] for h in range(HEADS)]
    return jnp.concatenate(
        [jnp.where(low_lane, cols[0], cols[1]), jnp.where(low_lane, cols[2], cols[3])], axis=1
    )


def head_reduce(values, kind):
    rows = values.shape[0]
    low_lane = lax.broadcasted_iota(jnp.int32, (rows, 128), 1) < 64
    fill = LOWEST if kind == "max" else 0.0
    cols = []
    for pair in range(2):
        part = values[:, pair * 128 : pair * 128 + 128]
        for keep_low in (True, False):
            picked = jnp.where(low_lane == keep_low, part, fill)
            if kind == "max":
                cols.append(jnp.max(picked, axis=1, keepdims=True))
            else:
                cols.append(jnp.sum(picked, axis=1, keepdims=True))
    return cols


def spread(cols):
    rows = cols[0].shape[0]
    low_lane = lax.broadcasted_iota(jnp.int32, (rows, 128), 1) < 64
    return jnp.concatenate(
        [jnp.where(low_lane, cols[0], cols[1]), jnp.where(low_lane, cols[2], cols[3])], axis=1
    )


def lanes_of(cols):
    rows = cols[0].shape[0]
    lane = lax.broadcasted_iota(jnp.int32, (rows, 128), 1)
    table = jnp.zeros((rows, 128), F32)
    for h, col in enumerate(cols):
        table = jnp.where(lane == h, col, table)
    return table


def pad_rows(values, rows):
    missing = rows - values.shape[0]
    if missing == 0:
        return values
    return jnp.concatenate([values, jnp.zeros((missing, values.shape[1]), values.dtype)], axis=0)


def self_weights(queries, keys, blocks, causal):
    k_blocks = [jnp.concatenate([k] * HEADS, axis=0) * blocks for k in keys]
    scores = [nt(q, kb) for q, kb in zip(queries, k_blocks)]
    weights = []
    for score in scores:
        score = jnp.where(causal, score * 0.125, LOWEST)
        top = spread(head_reduce(score, "max"))
        raised = jnp.where(causal, jnp.exp(score - top), 0.0)
        weights.append(raised / spread(head_reduce(raised, "sum")))
    return weights, k_blocks


class Names:
    pass


def layer_kernel(names, sizes, *refs):
    r = Names()
    for name, ref in zip(names, refs, strict=True):
        setattr(r, name, ref)
    rows, samples, slots, n_cond, n_dp, width = sizes
    hidden = r.dw.shape[0]
    part_rows = rows // NB
    own = part_rows // n_cond
    part_samples = samples // NB
    c = lax.axis_index("cond")
    d = lax.axis_index("dp")

    def peer(k):
        return (d, lax.rem(c + k, n_cond))

    core_peer = (d, c + 1 - 2 * lax.rem(c, 2))
    chip_peer = (d, lax.rem(c + 2, n_cond))
    bit0 = lax.rem(c, 2)
    bit1 = c // 2

    def row(k):
        return (lax.rem(d + k, n_dp), c)

    barrier = pltpu.get_barrier_semaphore()
    for k in range(1, n_cond):
        pl.semaphore_signal(barrier, inc=1, device_id=peer(k), device_id_type=MESH)
    for k in range(1, n_dp):
        pl.semaphore_signal(barrier, inc=1, device_id=row(k), device_id_type=MESH)

    loads = {}

    def load(name, src, dst, at):
        copy = pltpu.make_async_copy(src, dst, r.load_sem.at[at])
        copy.start()
        loads[name] = copy

    load("act", r.act_h, r.act, 0)
    load("rw", r.rw_h, r.rw, 1)
    load("vec", r.vec_h, r.vec, 2)
    load("mw", r.mw_h, r.mw, 3)
    mem_parts = 4
    mem_rows = samples * slots // mem_parts
    for i in range(mem_parts):
        span = pl.ds(i * mem_rows, mem_rows)
        load(f"mem{i}", r.mem_h.at[span], r.mem.at[span], 8 + i)
    load("mask", r.mask_h, r.mask, 4)
    load("flag", r.flag_h, r.flag, 5)
    load("dw", r.dw_h, r.dw, 6)
    load("cot", r.cot_h, r.cot, 7)

    lane256 = lax.broadcasted_iota(jnp.int32, (256, 256), 1)
    row256 = lax.broadcasted_iota(jnp.int32, (256, 256), 0)
    r.blocks[...] = half(jnp.where(lane256 // 64 == row256 // 64, 1.0, 0.0))
    lane64 = lax.broadcasted_iota(jnp.int32, (64, 256), 1)
    row64 = lax.broadcasted_iota(jnp.int32, (64, 256), 0)
    r.heads[...] = jnp.where(lane64 // 64 == row64 // 16, 1.0, 0.0)
    r.heads_b[...] = half(r.heads[...])

    def causal_mask():
        key = lax.rem(lane64, 64)
        return (key // H == row64 // H) & (key <= row64)

    loads["act"].wait()
    loads["rw"].wait()
    loads["vec"].wait()

    @pl.loop(0, 4)
    def _(i):
        span = pl.ds(pl.multiple_of(i * 64, 64), 64)
        r.rwb[span, :] = half(r.rw[span, :])

    def vec(i):
        return r.vec[i : i + 1, :]

    w_qkv = lambda: r.rwb[:, : 3 * width]
    w_so = lambda: r.rwb[:, 3 * width : 4 * width]
    w_cq = lambda: r.rwb[:, 4 * width : 5 * width]
    w_co = lambda: r.rwb[:, 5 * width : 6 * width]
    w_up = lambda: r.rwb[:, 6 * width :]

    def self_forward(b):
        group = 256

        @pl.loop(0, part_rows // group)
        def _(g):
            span = pl.ds(pl.multiple_of(b * part_rows + g * group, group), group)
            x = r.act[span, :]
            unit, _ = unit_rows(x)
            a1 = half(unit * vec(0) + vec(1))
            r.a1[span, :] = a1
            qkv = half(nn(a1, w_qkv()))
            r.qkv[span, :] = qkv
            causal = causal_mask()
            blocks = r.blocks[...]
            pieces = [qkv[s * 64 : s * 64 + 64, :] for s in range(group // 64)]
            q, k, v = ([p[:, i * width : (i + 1) * width] for p in pieces] for i in range(3))
            v_blocks = [jnp.concatenate([x] * HEADS, axis=0) * blocks for x in v]
            weights, _ = self_weights(q, k, blocks, causal)
            mixed = [nn(half(w), vb) for w, vb in zip(weights, v_blocks)]
            o1 = half(jnp.concatenate(mixed, axis=0))
            r.o1[span, :] = o1
            x1 = x + nn(o1, w_so())
            r.x1[span, :] = x1
            unit2, _ = unit_rows(x1)
            a2 = half(unit2 * vec(2) + vec(3))
            r.a2[span, :] = a2
            r.qs[span, :] = half(nn(a2, w_cq()) * 0.125)

    def pair_forward(b):
        batch = 8
        step = batch * slots

        @pl.loop(0, part_samples // batch)
        def _(g):
            first = b * part_samples + g * batch
            span = pl.ds(pl.multiple_of(first * slots, step), step)
            chunk = r.mem[span, :]
            for side in range(2):
                cols = slice(side * width, (side + 1) * width)
                kv = nn(chunk, r.mwb[:, cols])
                for s in range(batch):
                    r.kv[first + s, :, cols] = half(kv[s * slots : (s + 1) * slots, :])

    def usable_rows():
        position = lax.broadcasted_iota(jnp.int32, (samples, slots), 1)
        kept = (position < r.flag[...]) & (r.mask[...] == 1)
        time_token = (position == PATCHES) & (c == 0)
        r.use[...] = jnp.where(kept | time_token, 1.0, 0.0)

    def cross_forward(b):
        unroll = 16

        @pl.loop(0, part_samples // unroll)
        def _(g):
            picks = [b * part_samples + g * unroll + i for i in range(unroll)]
            spans = [pl.ds(pl.multiple_of(s * H, H), H) for s in picks]
            heads_b = r.heads_b[...]
            scores = []
            for s, span in zip(picks, spans):
                q = jnp.concatenate([r.qs[span, :]] * HEADS, axis=0) * heads_b
                scores.append(nt(q, r.kv[s, :, :width]))
            weights = []
            for s, span, score in zip(picks, spans, scores):
                usable = jnp.broadcast_to(r.use[pl.ds(s, 1), :], (64, slots)) > 0.5
                score = jnp.where(usable, score, LOWEST)
                top = jnp.max(score, axis=1, keepdims=True)
                raised = jnp.where(usable, jnp.exp(score - top), 0.0)
                total = jnp.sum(raised, axis=1, keepdims=True)
                p = half(raised)
                r.p[s] = p
                weights.append(p)
                r.top[span, :] = lanes_of([top[h * H : h * H + H, :] for h in range(HEADS)])
                r.total[span, :] = lanes_of([total[h * H : h * H + H, :] for h in range(HEADS)])
            mixes = [nn(p, r.kv[s, :, width:]) for s, p in zip(picks, weights)]
            for span, mixed in zip(spans, mixes):
                mixed = mixed * r.heads[...]
                r.o_out[span, :] = half(sum(mixed[h * H : h * H + H, :] for h in range(HEADS)))

    pending = []

    def send(src, dst, at, to):
        copy = pltpu.make_async_remote_copy(
            src_ref=src,
            dst_ref=dst,
            send_sem=r.ssem.at[at],
            recv_sem=r.rsem.at[at],
            device_id=to,
            device_id_type=MESH,
        )
        copy.start()
        pending.append(copy)
        return copy

    def own_span(b, owner):
        return pl.ds(pl.multiple_of(b * part_rows + owner * own, own), own)

    flights = {}

    def send_mixed(b):
        for k in range(n_cond):
            owner = lax.rem(c + k, n_cond)
            span = own_span(b, owner)
            stats = jnp.concatenate(
                [
                    pad_rows(r.top[span, :], 128).T[:8, :],
                    pad_rows(r.total[span, :], 128).T[:8, :],
                ],
                axis=0,
            )
            if k == 0:
                r.st_in[b, 0] = stats
                r.o_in[b, 0] = r.o_out[span, :]
            else:
                r.st_out[b, k] = stats
                at = (b * n_cond + k) * 2
                flights["o", b, k] = (
                    send(r.st_out.at[b, k], r.st_in.at[b, k], at, peer(k)),
                    send(r.o_out.at[span, :], r.o_in.at[b, k], at + 1, peer(k)),
                )

    def middle(b):
        mine = pl.ds(b * own, own)
        me = own_span(b, c)
        biases = hidden // width
        cot = r.cot[me, :]
        dz = half(cot)
        r.dz[mine, :] = dz
        grad_acts = [nt(dz, r.dwb[j * width : (j + 1) * width, :]) for j in range(biases)]
        for k in range(1, n_cond):
            for copy in flights["o", b, k]:
                copy.wait_recv()
        tops = [r.st_in[b, k, :8, :] for k in range(n_cond)]
        top = functools.reduce(jnp.maximum, tops)
        raised = [jnp.exp(t - top) for t in tops]
        total = sum(w * r.st_in[b, k, 8:, :] for k, w in enumerate(raised))
        total = jnp.maximum(total, 0.5)
        shares = [w / total for w in raised]
        table = pad_rows(jnp.concatenate(shares, axis=0), 128).T[:own, :]
        spreads = [head_columns(table, 8 * k) for k in range(n_cond)]
        o2 = sum(spreads[k] * wide(r.o_in[b, k]) for k in range(n_cond))
        o2b = half(o2)
        r.o2[mine, :] = o2b
        x2 = r.x1[me, :] + nn(o2b, w_co())
        unit, rate = unit_rows(x2)
        a3 = half(unit * vec(4) + vec(5))
        r.a3[mine, :] = a3
        ups = [slice(6 * width + j * width, 6 * width + (j + 1) * width) for j in range(biases)]
        downs = [slice(j * width, (j + 1) * width) for j in range(biases)]
        us = [nn(a3, r.rwb[:, cols]) for cols in ups]
        acts, slopes = [], []
        for j in range(biases):
            u = us[j] + vec(6 + j)
            below = 0.5 + 0.5 * lax.erf(u * (2.0**-0.5))
            acts.append(half(u * below))
            slopes.append(
                below + u * (jnp.exp(-0.5 * u * u) * (1.0 / math.sqrt(2.0 * math.pi)))
            )
        dus = []
        for j in range(biases):
            du = half(grad_acts[j] * slopes[j])
            r.du[mine, downs[j]] = du
            dus.append(du)
        da3 = sum(nt(du, r.rwb[:, cols]) for du, cols in zip(dus, ups))
        for j in range(biases):
            r.hb[mine, downs[j]] = acts[j]
            add_vec(b, 6 + j, column_sum(wide(dus[j])))
        out = x2 + vec(6 + biases)
        out = out + sum(nn(hb, r.dwb[here, :]) for hb, here in zip(acts, downs))
        r.out16[me, :] = half(out)
        add_vec(b, 6 + biases, column_sum(wide(dz)))
        add_vec(b, 4, column_sum(da3 * unit))
        add_vec(b, 5, column_sum(da3))
        dx2 = cot + unit_back(da3 * vec(4), unit, rate)
        r.dx2[mine, :] = dx2
        dy = half(dx2)
        r.dy2[mine, :] = dy
        do2 = wide(half(nt(dy, w_co())))
        delta = lanes_of(head_reduce(do2 * wide(o2b), "sum"))
        delta = pad_rows(delta, 128).T[:8, :]
        for k in range(n_cond):
            grads = half(do2 * spreads[k])
            dots = delta * shares[k]
            if k == 0:
                r.do_in[me, :] = grads
                r.dl_in[b, 0] = dots
            else:
                r.do_out[b, k] = grads
                r.dl_out[b, k] = dots
                at = (NB * n_cond + b * n_cond + k) * 2
                to = peer(n_cond - k)
                flights["do", b, k] = (
                    send(r.dl_out.at[b, k], r.dl_in.at[b, k], at, to),
                    send(r.do_out.at[b, k], r.do_in.at[me, :], at + 1, to),
                )

    def add_vec(b, i, values):
        if b == 0:
            r.vg[i : i + 1, :] = values
        else:
            r.vg[i : i + 1, :] += values

    def cross_backward(b):
        for k in range(n_cond):
            owner = lax.rem(c + k, n_cond)
            if k:
                for copy in flights["do", b, k]:
                    copy.wait_recv()
            r.dl[own_span(b, owner), :] = pad_rows(r.dl_in[b, k], 128).T[:own, :]
        unroll = 16

        @pl.loop(0, part_samples // unroll)
        def _(g):
            first = b * part_samples + g * unroll
            picks = [first + i for i in range(unroll)]
            spans = [pl.ds(pl.multiple_of(s * H, H), H) for s in picks]
            heads_b = r.heads_b[...]
            grads = [
                jnp.concatenate([r.do_in[span, :]] * HEADS, axis=0) * heads_b for span in spans
            ]
            raws = [nt(grad, r.kv[s, :, width:]) for s, grad in zip(picks, grads)]
            slopes = []
            for s, span, raw in zip(picks, spans, raws):
                dots = r.dl[span, :]
                dots = jnp.concatenate([dots[:, h : h + 1] for h in range(HEADS)], axis=0)
                slopes.append(half(wide(r.p[s]) * (raw - dots)))
            backs = [nn(ds, r.kv[s, :, :width]) for s, ds in zip(picks, slopes)]
            for span, dq in zip(spans, backs):
                dq = dq * r.heads[...]
                dq = sum(dq[h * H : h * H + H, :] for h in range(HEADS)) * 0.125
                r.dq_out[span, :] = half(dq)
            for pair in range(unroll // 2):
                keys, values = [], []
                for i in (2 * pair, 2 * pair + 1):
                    q = jnp.concatenate([r.qs[spans[i], :]] * HEADS, axis=0) * heads_b
                    keys.append(tn(slopes[i], q))
                    values.append(tn(r.p[picks[i]], grads[i]))
                span = pl.ds(
                    pl.multiple_of(first * slots + pair * 2 * slots, 2 * slots), 2 * slots
                )
                r.dkv[span, :width] = half(jnp.concatenate(keys, axis=0))
                r.dkv[span, width:] = half(jnp.concatenate(values, axis=0))

    def send_query_grads(b):
        for k in range(1, n_cond):
            owner = lax.rem(c + k, n_cond)
            at = 4 * NB * n_cond + b * n_cond + k
            flights["dq", b, k] = send(
                r.dq_out.at[own_span(b, owner), :], r.dq_in.at[b, k], at, peer(k)
            )

    def self_backward(b):
        me = own_span(b, c)
        mine = pl.ds(b * own, own)
        total = wide(r.dq_out[me, :])
        for k in range(1, n_cond):
            flights["dq", b, k].wait_recv()
            total = total + wide(r.dq_in[b, k])
        dqc = half(total)
        r.dqc[mine, :] = dqc
        da2 = nt(dqc, w_cq())
        unit2, rate2 = unit_rows(r.x1[me, :])
        add_vec(b, 2, column_sum(da2 * unit2))
        add_vec(b, 3, column_sum(da2))
        dx1 = r.dx2[mine, :] + unit_back(da2 * vec(2), unit2, rate2)
        dy1 = half(dx1)
        r.dy1[mine, :] = dy1
        do1 = half(nt(dy1, w_so()))
        causal = causal_mask()
        blocks = r.blocks[...]
        spans = [
            pl.ds(pl.multiple_of(b * part_rows + c * own + s * 64, 64), 64)
            for s in range(own // 64)
        ]
        q, k, v = (
            [r.qkv[span, i * width : (i + 1) * width] for span in spans] for i in range(3)
        )
        grads = [do1[s * 64 : s * 64 + 64, :] for s in range(own // 64)]
        v_blocks = [jnp.concatenate([x] * HEADS, axis=0) * blocks for x in v]
        dps = [nt(grad, vb) for grad, vb in zip(grads, v_blocks)]
        weights, k_blocks = self_weights(q, k, blocks, causal)
        pieces = []
        for i in range(own // 64):
            dv = tn(half(weights[i]), grads[i]) * wide(blocks)
            dots = spread(head_reduce(weights[i] * dps[i], "sum"))
            ds = half(weights[i] * (dps[i] - dots))
            dq = nn(ds, k_blocks[i]) * 0.125
            dk = tn(ds, q[i]) * wide(blocks)
            dk = sum(dk[h * 64 : h * 64 + 64, :] for h in range(HEADS)) * 0.125
            dv = sum(dv[h * 64 : h * 64 + 64, :] for h in range(HEADS))
            pieces.append(half(jnp.concatenate([dq, dk, dv], axis=1)))
        dqkv = jnp.concatenate(pieces, axis=0)
        r.dqkv[mine, :] = dqkv
        da1 = nt(dqkv, w_qkv())
        unit1, rate1 = unit_rows(r.act[me, :])
        add_vec(b, 0, column_sum(da1 * unit1))
        add_vec(b, 1, column_sum(da1))
        r.ga16[me, :] = half(dx1 + unit_back(da1 * vec(0), unit1, rate1))

    layout = {"ffn": (0, 2 * hidden), "row": (2 * hidden, 6 * width)}
    layout["pair"] = (2 * hidden + 6 * width, 2 * width)
    set_at = {name: 5 * NB * n_cond + 8 + 6 * i for i, name in enumerate(layout)}

    def owned(ref, dyn):
        return jnp.concatenate([ref[own_span(b, c), :] for b in range(NB)], axis=0)

    def ffn_grads():
        for j in range(hidden // width):
            here = slice(j * width, (j + 1) * width)
            r.g[j * width : (j + 1) * width, :] = half(tn(r.a3[...], r.du[:, here]))
            at = hidden + j * width
            r.g[at : at + width, :] = half(tn(r.hb[:, here], r.dz[...]))

    def put_row(j, values):
        first = layout["row"][0] + j * width
        r.g[first : first + width, :] = half(values)

    def row_grads():
        put_row(0, tn(r.o2[...], r.dy2[...]))
        put_row(1, tn(owned(r.a2, c), r.dqc[...]))
        put_row(2, tn(owned(r.o1, c), r.dy1[...]))
        a1 = owned(r.a1, c)
        for j in range(3):
            put_row(3 + j, tn(a1, r.dqkv[:, j * width : (j + 1) * width]))

    def pair_grads():
        step = 8 * slots
        r.gw[...] = jnp.zeros_like(r.gw)

        @pl.loop(0, samples // 8)
        def _(g):
            span = pl.ds(pl.multiple_of(g * step, step), step)
            r.gw[...] += tn(r.mem[span, :], r.dkv[span, :])

        first = layout["pair"][0]
        for side in range(2):
            r.g[first + side * width : first + (side + 1) * width, :] = half(
                r.gw[:, side * width : (side + 1) * width]
            )

    def set_sizes(name):
        first, count = layout[name]
        quarter = count // 4
        piece = max(16, quarter // n_dp)
        return first, count, count // 2, quarter, piece, quarter // piece

    def at_rows(start, count):
        return pl.ds(pl.multiple_of(start, 16), count)

    def reduce_core(name):
        first, count, two, four, piece, owners = set_sizes(name)
        flights[name, 0] = send(
            r.g.at[at_rows(first + (1 - bit0) * two, two), :],
            r.rc.at[at_rows(first // 2, two), :],
            set_at[name],
            core_peer,
        )

    def reduce_chip(name):
        first, count, two, four, piece, owners = set_sizes(name)
        flights[name, 0].wait_recv()
        base = first // 2
        for q in range(2):
            span = pl.ds(base + q * four, four)
            got = wide(r.rc[span, :]) + wide(
                r.g[at_rows(first + bit0 * two + q * four, four), :]
            )
            r.rc[span, :] = half(got)
        flights[name, 1] = send(
            r.rc.at[at_rows(base + (1 - bit1) * four, four), :],
            r.ry.at[pl.ds(first // 4, four), :],
            set_at[name] + 1,
            chip_peer,
        )

    def wait_bytes(name, stage, ref, count, which):
        view = ref.at[pl.ds(0, count), :]
        copy = pltpu.make_async_remote_copy(
            src_ref=view,
            dst_ref=view,
            send_sem=r.ssem.at[set_at[name] + stage],
            recv_sem=r.rsem.at[set_at[name] + stage],
            device_id=core_peer,
            device_id_type=MESH,
        )
        if which == "recv":
            copy.wait_recv()
        else:
            copy.wait_send()

    def start(src, dst, at, to):
        pltpu.make_async_remote_copy(
            src_ref=src,
            dst_ref=dst,
            send_sem=r.ssem.at[at],
            recv_sem=r.rsem.at[at],
            device_id=to,
            device_id_type=MESH,
        ).start()

    def guard(full, cond, body):
        if full:
            body()
        else:
            pl.when(cond)(body)

    def reduce_rows(name):
        first, count, two, four, piece, owners = set_sizes(name)
        flights[name, 1].wait_recv()
        base = first // 4
        mine = wide(r.rc[at_rows(first // 2 + bit1 * four, four), :])
        span = pl.ds(base, four)
        r.ry[span, :] = half(mine + wide(r.ry[span, :]))
        for k in range(1, n_dp):
            to = lax.rem(d + k, n_dp)

            def go(k=k, to=to):
                start(
                    r.ry.at[at_rows(base + to * piece, piece), :],
                    r_rd(name).at[pl.ds(k * piece, piece), :],
                    set_at[name] + 2,
                    row(k),
                )

            guard(owners == n_dp, to < owners, go)

    def r_rd(name):
        return getattr(r, "rd_" + name)

    def quarter_at(name):
        first, count, two, four, piece, owners = set_sizes(name)
        return first + bit0 * two + bit1 * four

    def gather_rows(name):
        first, count, two, four, piece, owners = set_sizes(name)
        base = first // 4

        def finish():
            wait_bytes(name, 2, r_rd(name), (n_dp - 1) * piece, "recv")
            total = wide(r.ry[at_rows(base + d * piece, piece), :])
            for k in range(1, n_dp):
                total = total + wide(r_rd(name)[k * piece : (k + 1) * piece, :])
            here = at_rows(quarter_at(name) + d * piece, piece)
            r.tot[here, :] = half(total)
            for k in range(1, n_dp):
                start(r.tot.at[here, :], r.tot.at[here, :], set_at[name] + 3, row(k))

        guard(owners == n_dp, d < owners, finish)

    def gather_chip(name):
        first, count, two, four, piece, owners = set_sizes(name)
        if owners == n_dp:
            wait_bytes(name, 3, r.tot, (n_dp - 1) * piece, "recv")
        else:
            pl.when(d < owners)(
                lambda: wait_bytes(name, 3, r.tot, (owners - 1) * piece, "recv")
            )
            pl.when(d >= owners)(lambda: wait_bytes(name, 3, r.tot, owners * piece, "recv"))
        span = at_rows(quarter_at(name), four)
        flights[name, 4] = send(
            r.tot.at[span, :], r.tot.at[span, :], set_at[name] + 4, chip_peer
        )

    def gather_core(name):
        first, count, two, four, piece, owners = set_sizes(name)
        flights[name, 4].wait_recv()
        span = at_rows(first + bit0 * two, two)
        flights[name, 5] = send(
            r.tot.at[span, :], r.tot.at[span, :], set_at[name] + 5, core_peer
        )

    def end_set(name):
        first, count, two, four, piece, owners = set_sizes(name)
        flights[name, 5].wait_recv()
        if owners == n_dp:
            wait_bytes(name, 2, r.ry, (n_dp - 1) * piece, "send")
            wait_bytes(name, 3, r.tot, (n_dp - 1) * piece, "send")
        else:
            pl.when(d < owners)(
                lambda: wait_bytes(name, 2, r.ry, (owners - 1) * piece, "send")
            )
            pl.when(d >= owners)(lambda: wait_bytes(name, 2, r.ry, owners * piece, "send"))
            pl.when(d < owners)(lambda: wait_bytes(name, 3, r.tot, (n_dp - 1) * piece, "send"))

    vec_at = 5 * NB * n_cond + 8 + 6 * len(layout)

    def small_cond():
        r.vc_in[pl.ds(c, 1)] = r.vg[...][None]
        for k in range(1, n_cond):
            flights["vc", k] = send(r.vg, r.vc_in.at[c], vec_at + k - 1, peer(k))

    def small_rows():
        for k in range(1, n_cond):
            flights["vc", k].wait_recv()
        r.vd_in[pl.ds(d, 1)] = sum(r.vc_in[k] for k in range(n_cond))[None]
        for k in range(1, n_dp):
            start(r.vd_in.at[d], r.vd_in.at[d], vec_at + 3, row(k))

    def small_wait(which):
        view = r.vd_in.at[pl.ds(0, n_dp - 1)]
        copy = pltpu.make_async_remote_copy(
            src_ref=view,
            dst_ref=view,
            send_sem=r.ssem.at[vec_at + 3],
            recv_sem=r.rsem.at[vec_at + 3],
            device_id=core_peer,
            device_id_type=MESH,
        )
        copy.wait_recv() if which == "recv" else copy.wait_send()

    def small_end():
        small_wait("recv")
        total = r.vd_in[0]
        for k in range(1, n_dp):
            total = total + r.vd_in[k]
        r.vtot[...] = total
        small_wait("send")

    def share(name, ref, b):
        span = own_span(b, c)
        for k in range(1, n_cond):
            flights[name, b, k] = send(
                ref.at[span, :], ref.at[span, :], vec_at + 4 + len(shared), peer(k)
            )
            shared.append((name, b, k))

    shared = []

    r.vg[11:16, :] = jnp.zeros((5, width), F32)
    self_forward(0)
    loads["mw"].wait()
    r.mwb[...] = half(r.mw[...])
    loads["mask"].wait()
    loads["flag"].wait()
    usable_rows()
    for i in range(mem_parts // NB):
        loads[f"mem{i}"].wait()
    pair_forward(0)
    cross_forward(0)
    pl.semaphore_wait(barrier, n_cond - 1 + n_dp - 1)
    send_mixed(0)
    loads["dw"].wait()
    r.dwb[...] = half(r.dw[...])
    loads["cot"].wait()
    for b in range(1, NB):
        self_forward(b)
        for i in range(b * mem_parts // NB, (b + 1) * mem_parts // NB):
            loads[f"mem{i}"].wait()
        pair_forward(b)
        cross_forward(b)
        send_mixed(b)
    for b in range(NB):
        middle(b)
    ffn_grads()
    reduce_core("ffn")
    for b in range(NB):
        cross_backward(b)
        send_query_grads(b)
        if b == 0:
            reduce_chip("ffn")
        if b == NB - 1:
            reduce_rows("ffn")
    pair_grads()
    reduce_core("pair")
    for b in range(NB):
        self_backward(b)
        if b == 0:
            reduce_chip("pair")
            gather_rows("ffn")
    small_cond()
    row_grads()
    reduce_core("row")
    reduce_rows("pair")
    gather_chip("ffn")
    reduce_chip("row")
    small_rows()
    gather_rows("pair")
    reduce_rows("row")
    for b in range(NB):
        share("out16", r.out16, b)
        share("ga16", r.ga16, b)
    gather_core("ffn")
    gather_chip("pair")
    gather_rows("row")
    gather_core("pair")
    gather_chip("row")
    gather_core("row")
    small_end()
    for key in shared:
        flights[key].wait_recv()
    for name in layout:
        end_set(name)
    for copy in pending:
        copy.wait_send()


def step_kernel(names, token_count, *refs):
    r = Names()
    for name, ref in zip(names, refs, strict=True):
        setattr(r, name, ref)
    width = r.w_p.shape[0]
    hidden = r.w_d.shape[0]
    keep = 1.0 - (1.0 + STEP) ** (-0.75)
    copies = []

    def store(src, dst):
        copy = pltpu.make_async_copy(src, dst, r.sem.at[len(copies)])
        copy.start()
        copies.append(copy)

    r.mwb[...] = half(r.w_p[...])
    total_rows = r.dkv.shape[0]
    chunks = 8
    step = total_rows // chunks
    for i in range(chunks):
        inner = 2
        small = step // inner

        @pl.loop(0, inner)
        def _(j, i=i):
            span = pl.ds(pl.multiple_of(i * step + j * small, 16), small)
            r.gm[span, :] = nt(r.dkv[span, :], r.mwb[...])

        span = pl.ds(i * step, step)
        store(r.gm.at[span, :], r.gm_h.at[span, :])
    r.out[...] = wide(r.out16[...])
    store(r.out, r.out_h)
    r.ga[...] = wide(r.ga16[...])
    store(r.ga, r.ga_h)

    def update(weight, grad, moment, average):
        scaled = grad / token_count
        moment_new = INERTIA * moment + scaled
        weight_new = weight - STEP_RATE * (scaled + INERTIA * moment_new)
        average_new = keep * average + (1.0 - keep) * weight_new
        return moment_new, weight_new, average_new

    def group(prefix, views):
        w, m, a = (getattr(r, kind + "_" + prefix) for kind in "wma")
        for rows, cols, grad in views:
            new = update(w[rows, cols], grad(), m[rows, cols], a[rows, cols])
            for kind, value in zip("mwa", new):
                getattr(r, prefix + kind)[rows, cols] = value
        for kind in "mwa":
            store(getattr(r, prefix + kind), getattr(r, prefix + kind + "_h"))

    every = slice(None)
    row_first = 2 * hidden
    pair_first = row_first + 6 * width
    order = {5: 0, 4: 1, 3: 2, 0: 3, 1: 4, 2: 5}

    def table(first):
        return lambda: wide(r.tot[first : first + width, :])

    group(
        "d",
        [
            (slice(j * width, (j + 1) * width), every, table(hidden + j * width))
            for j in range(hidden // width)
        ],
    )
    group(
        "r",
        [
            (every, slice(j * width, (j + 1) * width), table(row_first + order[j] * width))
            for j in range(6)
        ]
        + [
            (every, slice((6 + j) * width, (7 + j) * width), table(j * width))
            for j in range(hidden // width)
        ],
    )
    group(
        "p",
        [
            (every, slice(j * width, (j + 1) * width), table(pair_first + j * width))
            for j in range(2)
        ],
    )
    group("v", [(every, every, lambda: r.vtot[: r.w_v.shape[0], :])])
    for copy in copies:
        copy.wait()


def per_device(
    actions,
    memory,
    patch_flags,
    memory_mask,
    cotangent,
    row_weights,
    memory_weights,
    down_weight,
    vectors,
    row_momentum,
    memory_momentum,
    down_momentum,
    vector_momentum,
    row_average,
    memory_average,
    down_average,
    vector_average,
):
    rows, width = actions.shape
    samples = rows // H
    slots = memory.shape[1]
    hidden = down_weight.shape[0]
    n_cond = lax.axis_size("cond")
    n_dp = lax.axis_size("dp")
    part_rows = rows // NB
    own = part_rows // n_cond
    total = 2 * hidden + 8 * width
    flat = samples * slots
    ins = {
        "act_h": actions,
        "mem_h": memory.reshape(flat, width),
        "mask_h": memory_mask,
        "flag_h": patch_flags,
        "cot_h": cotangent,
        "rw_h": row_weights,
        "mw_h": memory_weights,
        "dw_h": down_weight,
        "vec_h": vectors,
    }
    outs = {
        "tot": ((total, width), BF),
        "vtot": ((16, width), F32),
        "dkv": ((flat, 2 * width), BF),
        "out16": ((rows, width), BF),
        "ga16": ((rows, width), BF),
    }

    def pieces(count):
        return n_dp * max(16, count // 4 // n_dp)

    scratch = {
        "act": ((rows, width), F32),
        "rw": (row_weights.shape, F32),
        "vec": (vectors.shape, F32),
        "mw": (memory_weights.shape, F32),
        "mem": ((flat, width), BF),
        "mask": (memory_mask.shape, jnp.int32),
        "flag": (patch_flags.shape, jnp.int32),
        "dw": (down_weight.shape, F32),
        "cot": ((rows, width), F32),
        "rwb": (row_weights.shape, BF),
        "mwb": (memory_weights.shape, BF),
        "dwb": (down_weight.shape, BF),
        "blocks": ((256, 256), BF),
        "heads": ((64, 256), F32),
        "heads_b": ((64, 256), BF),
        "a1": ((rows, width), BF),
        "qkv": ((rows, 3 * width), BF),
        "o1": ((rows, width), BF),
        "x1": ((rows, width), F32),
        "a2": ((rows, width), BF),
        "qs": ((rows, width), BF),
        "kv": ((samples, slots, 2 * width), BF),
        "use": ((samples, slots), F32),
        "p": ((samples, 64, slots), BF),
        "o_out": ((rows, width), BF),
        "top": ((rows, 128), F32),
        "total": ((rows, 128), F32),
        "st_in": ((NB, n_cond, 16, 128), F32),
        "st_out": ((NB, n_cond, 16, 128), F32),
        "o_in": ((NB, n_cond, own, width), BF),
        "o2": ((NB * own, width), BF),
        "a3": ((NB * own, width), BF),
        "dz": ((NB * own, width), BF),
        "hb": ((NB * own, hidden), BF),
        "du": ((NB * own, hidden), BF),
        "dx2": ((NB * own, width), F32),
        "dy2": ((NB * own, width), BF),
        "dqc": ((NB * own, width), BF),
        "dy1": ((NB * own, width), BF),
        "dqkv": ((NB * own, 3 * width), BF),
        "do_in": ((rows, width), BF),
        "do_out": ((NB, n_cond, own, width), BF),
        "dl_in": ((NB, n_cond, 8, 128), F32),
        "dl_out": ((NB, n_cond, 8, 128), F32),
        "dl": ((rows, 128), F32),
        "dq_out": ((rows, width), BF),
        "dq_in": ((NB, n_cond, own, width), BF),
        "vg": ((16, width), F32),
        "vc_in": ((n_cond, 16, width), F32),
        "vd_in": ((n_dp, 16, width), F32),
        "g": ((total, width), BF),
        "gw": ((width, 2 * width), F32),
        "rc": ((total // 2, width), BF),
        "ry": ((total // 4, width), BF),
        "rd_ffn": ((pieces(2 * hidden), width), BF),
        "rd_row": ((pieces(6 * width), width), BF),
        "rd_pair": ((pieces(2 * width), width), BF),
    }
    sems = {
        "load_sem": pltpu.SemaphoreType.DMA((16,)),
        "ssem": pltpu.SemaphoreType.DMA((96,)),
        "rsem": pltpu.SemaphoreType.DMA((96,)),
    }
    whole = pl.BlockSpec(memory_space=pltpu.VMEM)
    far = pl.BlockSpec(memory_space=pltpu.HBM)
    names = list(ins) + list(outs) + list(scratch) + list(sems)
    sizes = (rows, samples, slots, n_cond, n_dp, width)
    tot, vtot, dkv, out16, ga16 = pl.pallas_call(
        functools.partial(layer_kernel, names, sizes),
        out_shape=[jax.ShapeDtypeStruct(*v) for v in outs.values()],
        in_specs=[far] * len(ins),
        out_specs=[whole] * len(outs),
        scratch_shapes=[pltpu.VMEM(*v) for v in scratch.values()] + list(sems.values()),
        compiler_params=pltpu.CompilerParams(
            collective_id=0, has_side_effects=True, vmem_limit_bytes=32 * MIB
        ),
        name="layer",
    )(*(pltpu.with_memory_space_constraint(v, pltpu.HBM) for v in ins.values()))

    ins2 = {
        "tot": tot,
        "vtot": vtot,
        "dkv": dkv,
        "out16": out16,
        "ga16": ga16,
        "w_r": row_weights,
        "w_p": memory_weights,
        "w_d": down_weight,
        "w_v": vectors,
        "m_r": row_momentum,
        "m_p": memory_momentum,
        "m_d": down_momentum,
        "m_v": vector_momentum,
        "a_r": row_average,
        "a_p": memory_average,
        "a_d": down_average,
        "a_v": vector_average,
    }
    outs2 = {
        "out": (rows, width),
        "ga": (rows, width),
        "gm": (flat, width),
    }
    for prefix, array in (("r", row_weights), ("p", memory_weights), ("d", down_weight), ("v", vectors)):
        for kind in "mwa":
            outs2[prefix + kind] = array.shape
    names2 = list(ins2) + [k + "_h" for k in outs2] + list(outs2) + ["mwb", "sem"]
    results = pl.pallas_call(
        functools.partial(step_kernel, names2, float(rows * n_dp)),
        out_shape=[jax.ShapeDtypeStruct(v, F32) for v in outs2.values()],
        in_specs=[whole] * len(ins2),
        out_specs=[far] * len(outs2),
        scratch_shapes=[pltpu.VMEM(v, F32) for v in outs2.values()]
        + [pltpu.VMEM(memory_weights.shape, BF), pltpu.SemaphoreType.DMA((32,))],
        compiler_params=pltpu.CompilerParams(vmem_limit_bytes=26 * MIB),
        name="step",
    )(*ins2.values())
    out, ga, gm = results[:3]
    return (out, ga, gm.reshape(samples, slots, width), *results[3:])


def solution(mesh):
    in_specs = (
        P("dp", None),
        P("dp", "cond", None),
        P("dp", "cond"),
        P("dp", "cond"),
        P("dp", None),
    ) + (P(),) * 12
    out_specs = (P("dp", None), P("dp", None), P("dp", "cond", None)) + (P(),) * 12
    return jax.shard_map(
        per_device, mesh=mesh, in_specs=in_specs, out_specs=out_specs, check_vma=False
    )
```

```python
import functools
import math

import jax
import jax.numpy as jnp
from jax import lax
from jax.experimental import pallas as pl
from jax.experimental.pallas import tpu as pltpu
from jax.sharding import PartitionSpec as P

HEADS = 4
H = 16
PATCHES = 196
STEP = 10
INERTIA = 0.9
STEP_RATE = 1.0
LOWEST = -1e30
NB = 2
MESH = pl.DeviceIdType.MESH
MIB = 2**20
BF = jnp.bfloat16
F32 = jnp.float32


def half(values):
    return values.astype(BF)


def wide(values):
    return values.astype(F32)


def nn(a, b):
    return jnp.dot(a, b, preferred_element_type=F32)


def nt(a, b):
    return lax.dot_general(a, b, (((1,), (1,)), ((), ())), preferred_element_type=F32)


def tn(a, b):
    return lax.dot_general(a, b, (((0,), (0,)), ((), ())), preferred_element_type=F32)


def unit_rows(values):
    centered = values - jnp.mean(values, axis=-1, keepdims=True)
    rate = lax.rsqrt(jnp.mean(centered * centered, axis=-1, keepdims=True) + 1e-05)
    return centered * rate, rate


def unit_back(grad, unit, rate):
    return rate * (
        grad
        - jnp.mean(grad, axis=-1, keepdims=True)
        - unit * jnp.mean(grad * unit, axis=-1, keepdims=True)
    )


def column_sum(values):
    return jnp.sum(values, axis=0, keepdims=True)


def head_columns(table, first):
    rows = table.shape[0]
    low_lane = lax.broadcasted_iota(jnp.int32, (rows, 128), 1) < 64
    cols = [table[:, first + h : first + h + 1] for h in range(HEADS)]
    return jnp.concatenate(
        [jnp.where(low_lane, cols[0], cols[1]), jnp.where(low_lane, cols[2], cols[3])], axis=1
    )


def head_reduce(values, kind):
    rows = values.shape[0]
    low_lane = lax.broadcasted_iota(jnp.int32, (rows, 128), 1) < 64
    fill = LOWEST if kind == "max" else 0.0
    cols = []
    for pair in range(2):
        part = values[:, pair * 128 : pair * 128 + 128]
        for keep_low in (True, False):
            picked = jnp.where(low_lane == keep_low, part, fill)
            if kind == "max":
                cols.append(jnp.max(picked, axis=1, keepdims=True))
            else:
                cols.append(jnp.sum(picked, axis=1, keepdims=True))
    return cols


def spread(cols):
    rows = cols[0].shape[0]
    low_lane = lax.broadcasted_iota(jnp.int32, (rows, 128), 1) < 64
    return jnp.concatenate(
        [jnp.where(low_lane, cols[0], cols[1]), jnp.where(low_lane, cols[2], cols[3])], axis=1
    )


def lanes_of(cols):
    rows = cols[0].shape[0]
    lane = lax.broadcasted_iota(jnp.int32, (rows, 128), 1)
    table = jnp.zeros((rows, 128), F32)
    for h, col in enumerate(cols):
        table = jnp.where(lane == h, col, table)
    return table


def pad_rows(values, rows):
    missing = rows - values.shape[0]
    if missing == 0:
        return values
    return jnp.concatenate([values, jnp.zeros((missing, values.shape[1]), values.dtype)], axis=0)


def self_weights(queries, keys, blocks, causal, beside=lambda: None):
    k_blocks = [jnp.concatenate([k] * HEADS, axis=0) * blocks for k in keys]
    scores = [nt(q, kb) for q, kb in zip(queries, k_blocks)]
    beside()
    weights = []
    for score in scores:
        score = jnp.where(causal, score * 0.125, LOWEST)
        top = spread(head_reduce(score, "max"))
        raised = jnp.where(causal, jnp.exp(score - top), 0.0)
        weights.append(raised / spread(head_reduce(raised, "sum")))
    return weights, k_blocks


class Names:
    pass


def layer_kernel(names, sizes, *refs):
    r = Names()
    for name, ref in zip(names, refs, strict=True):
        setattr(r, name, ref)
    rows, samples, slots, n_cond, n_dp, width = sizes
    hidden = r.dw.shape[0]
    part_rows = rows // NB
    own = part_rows // n_cond
    part_samples = samples // NB
    c = lax.axis_index("cond")
    d = lax.axis_index("dp")

    def peer(k):
        return (d, lax.rem(c + k, n_cond))

    core = lax.rem(c, 2)
    side_x = lax.rem(d, 2)
    side_y = c // 2
    plane = side_x + 2 * side_y
    line = d // 2
    n_line = n_dp // 2
    core_peer = (d, c + 1 - 2 * core)
    chip_peer = (d, lax.rem(c + 2, n_cond))

    def plane_place(k):
        x = 1 - side_x if k & 1 else side_x
        y = 1 - side_y if k & 2 else side_y
        return x + 2 * y

    def plane_peer(k):
        return (
            d + 1 - 2 * side_x if k & 1 else d,
            lax.rem(c + 2, n_cond) if k & 2 else c,
        )

    def line_place(k):
        return lax.rem(line + k, n_line)

    def line_peer(k):
        return (2 * line_place(k) + side_x, c)

    barrier = pltpu.get_barrier_semaphore()
    friends = [peer(k) for k in range(1, n_cond)]
    friends += [plane_peer(k) for k in (1, 3)]
    friends += [line_peer(k) for k in range(1, n_line)]
    for friend in friends:
        pl.semaphore_signal(barrier, inc=1, device_id=friend, device_id_type=MESH)

    loads = {}

    def load(name, src, dst, at):
        copy = pltpu.make_async_copy(src, dst, r.load_sem.at[at])
        copy.start()
        loads[name] = copy

    mem_parts = 4
    mem_rows = samples * slots // mem_parts

    def load_memory(i):
        span = pl.ds(i * mem_rows, mem_rows)
        load(f"mem{i}", r.mem_h.at[span], r.mem.at[span], 8 + i)

    load("mw", r.mw_h, r.mw, 3)
    load_memory(0)
    load("act", r.act_h, r.act, 0)
    load("vec", r.vec_h, r.vec, 2)
    load("rw", r.rw_h, r.rw, 1)
    load_memory(1)
    load("mask", r.mask_h, r.mask, 4)
    load("flag", r.flag_h, r.flag, 5)
    load("dw", r.dw_h, r.dw, 6)
    load("cot", r.cot_h, r.cot, 7)
    load_memory(2)
    load_memory(3)

    def load_moments():
        for i, name in enumerate(("m_r", "m_d", "m_p", "a_r", "a_d", "a_p")):
            load(name, getattr(r, name + "_h"), getattr(r, name), 16 + i)

    lane256 = lax.broadcasted_iota(jnp.int32, (256, 256), 1)
    row256 = lax.broadcasted_iota(jnp.int32, (256, 256), 0)
    r.blocks[...] = half(jnp.where(lane256 // 64 == row256 // 64, 1.0, 0.0))
    lane64 = lax.broadcasted_iota(jnp.int32, (64, 256), 1)
    row64 = lax.broadcasted_iota(jnp.int32, (64, 256), 0)
    r.heads[...] = jnp.where(lane64 // 64 == row64 // 16, 1.0, 0.0)
    r.heads_b[...] = half(r.heads[...])

    def causal_mask():
        key = lax.rem(lane64, 64)
        return (key // H == row64 // H) & (key <= row64)

    def vec(i):
        return r.vec[i : i + 1, :]

    w_qkv = lambda: r.rwb[:, : 3 * width]
    w_so = lambda: r.rwb[:, 3 * width : 4 * width]
    w_cq = lambda: r.rwb[:, 4 * width : 5 * width]
    w_co = lambda: r.rwb[:, 5 * width : 6 * width]
    w_up = lambda: r.rwb[:, 6 * width :]

    def pair_forward(first):
        span = pl.ds(pl.multiple_of(first * slots, 2 * slots), 2 * slots)
        kv = nn(r.mem[span, :], r.mwb[...])
        for s in range(2):
            r.kv[first + s] = half(kv[s * slots : (s + 1) * slots, :])

    def first_forward(b, waiting):
        def fill(count):
            for _ in range(min(count, len(waiting))):
                pair_forward(waiting.pop(0))

        span = pl.ds(b * part_rows, part_rows)
        x = r.act[span, :]
        unit, _ = unit_rows(x)
        a1 = half(unit * vec(0) + vec(1))
        r.a1[span, :] = a1
        fill(1)
        qkv = half(nn(a1, w_qkv()))
        r.qkv[span, :] = qkv
        fill(1)
        causal = causal_mask()
        blocks = r.blocks[...]
        pieces = [qkv[s * 64 : s * 64 + 64, :] for s in range(part_rows // 64)]
        q, k, v = ([p[:, i * width : (i + 1) * width] for p in pieces] for i in range(3))
        v_blocks = [jnp.concatenate([x] * HEADS, axis=0) * blocks for x in v]
        weights, _ = self_weights(q, k, blocks, causal, lambda: fill(2))
        mixed = [nn(half(w), vb) for w, vb in zip(weights, v_blocks)]
        o1 = half(jnp.concatenate(mixed, axis=0))
        r.o1[span, :] = o1
        fill(1)
        x1 = x + nn(o1, w_so())
        r.x1[span, :] = x1
        fill(2)
        unit2, _ = unit_rows(x1)
        a2 = half(unit2 * vec(2) + vec(3))
        r.a2[span, :] = a2
        r.qs[span, :] = half(nn(a2, w_cq()) * 0.125)
        fill(len(waiting))

    def usable_rows():
        position = lax.broadcasted_iota(jnp.int32, (samples, slots), 1)
        square = (samples, samples)
        diagonal = lax.broadcasted_iota(jnp.int32, square, 0) == lax.broadcasted_iota(
            jnp.int32, square, 1
        )
        counts = jnp.where(diagonal, jnp.broadcast_to(r.flag[...], square), 0)
        counts = jnp.sum(counts.astype(F32), axis=1, keepdims=True)
        kept = (position.astype(F32) < counts) & (r.mask[...] == 1)
        time_token = (position == PATCHES) & (c == 0)
        r.use[...] = jnp.where(kept | time_token, 1.0, 0.0)

    def cross_forward(b):
        unroll = 16

        @pl.loop(0, part_samples // unroll)
        def _(g):
            picks = [b * part_samples + g * unroll + i for i in range(unroll)]
            spans = [pl.ds(pl.multiple_of(s * H, H), H) for s in picks]
            heads_b = r.heads_b[...]
            scores = []
            for s, span in zip(picks, spans):
                q = jnp.concatenate([r.qs[span, :]] * HEADS, axis=0) * heads_b
                scores.append(nt(q, r.kv[s, :, :width]))
            weights = []
            for s, span, score in zip(picks, spans, scores):
                usable = jnp.broadcast_to(r.use[pl.ds(s, 1), :], (64, slots)) > 0.5
                score = jnp.where(usable, score, LOWEST)
                top = jnp.max(score, axis=1, keepdims=True)
                raised = jnp.where(usable, jnp.exp(score - top), 0.0)
                total = jnp.sum(raised, axis=1, keepdims=True)
                p = half(raised)
                r.p[s] = p
                weights.append(p)
                r.top[span, :] = lanes_of([top[h * H : h * H + H, :] for h in range(HEADS)])
                r.total[span, :] = lanes_of([total[h * H : h * H + H, :] for h in range(HEADS)])
            mixes = [nn(p, r.kv[s, :, width:]) for s, p in zip(picks, weights)]
            for span, mixed in zip(spans, mixes):
                mixed = mixed * r.heads[...]
                r.o_out[span, :] = half(sum(mixed[h * H : h * H + H, :] for h in range(HEADS)))

    pending = []

    def send(src, dst, at, to):
        copy = pltpu.make_async_remote_copy(
            src_ref=src,
            dst_ref=dst,
            send_sem=r.ssem.at[at],
            recv_sem=r.rsem.at[at],
            device_id=to,
            device_id_type=MESH,
        )
        copy.start()
        pending.append(copy)
        return copy

    def own_span(b, owner):
        return pl.ds(pl.multiple_of(b * part_rows + owner * own, own), own)

    flights = {}

    def send_mixed(b):
        for k in range(n_cond):
            owner = lax.rem(c + k, n_cond)
            span = own_span(b, owner)
            stats = jnp.concatenate(
                [
                    pad_rows(r.top[span, :], 128).T[:8, :],
                    pad_rows(r.total[span, :], 128).T[:8, :],
                ],
                axis=0,
            )
            if k == 0:
                r.st_in[b, 0] = stats
                r.o_in[b, 0] = r.o_out[span, :]
            else:
                r.st_out[b, k] = stats
                at = (b * n_cond + k) * 2
                flights["o", b, k] = (
                    send(r.st_out.at[b, k], r.st_in.at[b, k], at, peer(k)),
                    send(r.o_out.at[span, :], r.o_in.at[b, k], at + 1, peer(k)),
                )

    def middle(b):
        mine = pl.ds(b * own, own)
        me = own_span(b, c)
        biases = hidden // width
        cot = r.cot[me, :]
        dz = half(cot)
        r.dz[mine, :] = dz
        grad_acts = [nt(dz, r.dwb[j * width : (j + 1) * width, :]) for j in range(biases)]
        for k in range(1, n_cond):
            for copy in flights["o", b, k]:
                copy.wait_recv()
        tops = [r.st_in[b, k, :8, :] for k in range(n_cond)]
        top = functools.reduce(jnp.maximum, tops)
        raised = [jnp.exp(t - top) for t in tops]
        total = sum(w * r.st_in[b, k, 8:, :] for k, w in enumerate(raised))
        total = jnp.maximum(total, 0.5)
        shares = [w / total for w in raised]
        table = pad_rows(jnp.concatenate(shares, axis=0), 128).T[:own, :]
        spreads = [head_columns(table, 8 * k) for k in range(n_cond)]
        o2 = sum(spreads[k] * wide(r.o_in[b, k]) for k in range(n_cond))
        o2b = half(o2)
        r.o2[mine, :] = o2b
        x2 = r.x1[me, :] + nn(o2b, w_co())
        unit, rate = unit_rows(x2)
        a3 = half(unit * vec(4) + vec(5))
        r.a3[mine, :] = a3
        ups = [slice(6 * width + j * width, 6 * width + (j + 1) * width) for j in range(biases)]
        downs = [slice(j * width, (j + 1) * width) for j in range(biases)]
        us = [nn(a3, r.rwb[:, cols]) for cols in ups]
        acts, slopes = [], []
        for j in range(biases):
            u = us[j] + vec(6 + j)
            below = 0.5 + 0.5 * lax.erf(u * (2.0**-0.5))
            acts.append(half(u * below))
            slopes.append(
                below + u * (jnp.exp(-0.5 * u * u) * (1.0 / math.sqrt(2.0 * math.pi)))
            )
        dus = []
        for j in range(biases):
            du = half(grad_acts[j] * slopes[j])
            r.du[mine, downs[j]] = du
            dus.append(du)
        da3 = sum(nt(du, r.rwb[:, cols]) for du, cols in zip(dus, ups))
        dx2 = cot + unit_back(da3 * vec(4), unit, rate)
        r.dx2[mine, :] = dx2
        dy = half(dx2)
        r.dy2[mine, :] = dy
        do2 = wide(half(nt(dy, w_co())))
        delta = lanes_of(head_reduce(do2 * wide(o2b), "sum"))
        delta = pad_rows(delta, 128).T[:8, :]
        for k in range(n_cond):
            grads = half(do2 * spreads[k])
            dots = delta * shares[k]
            if k == 0:
                r.do_in[me, :] = grads
                r.dl_in[b, 0] = dots
            else:
                r.do_out[b, k] = grads
                r.dl_out[b, k] = dots
                at = (NB * n_cond + b * n_cond + k) * 2
                to = peer(n_cond - k)
                flights["do", b, k] = (
                    send(r.dl_out.at[b, k], r.dl_in.at[b, k], at, to),
                    send(r.do_out.at[b, k], r.do_in.at[me, :], at + 1, to),
                )
        for j in range(biases):
            r.hb[mine, downs[j]] = acts[j]
            add_vec(b, 6 + j, column_sum(wide(dus[j])))
        out = x2 + vec(6 + biases)
        out = out + sum(nn(hb, r.dwb[here, :]) for hb, here in zip(acts, downs))
        r.out16[me, :] = half(out)
        add_vec(b, 6 + biases, column_sum(wide(dz)))
        add_vec(b, 4, column_sum(da3 * unit))
        add_vec(b, 5, column_sum(da3))

    def add_vec(b, i, values):
        if b == 0:
            r.vg[i : i + 1, :] = values
        else:
            r.vg[i : i + 1, :] += values

    def cross_backward(b):
        for k in range(n_cond):
            owner = lax.rem(c + k, n_cond)
            if k:
                for copy in flights["do", b, k]:
                    copy.wait_recv()
            r.dl[own_span(b, owner), :] = pad_rows(r.dl_in[b, k], 128).T[:own, :]
        unroll = 16

        @pl.loop(0, part_samples // unroll)
        def _(g):
            first = b * part_samples + g * unroll
            picks = [first + i for i in range(unroll)]
            spans = [pl.ds(pl.multiple_of(s * H, H), H) for s in picks]
            heads_b = r.heads_b[...]
            grads = [
                jnp.concatenate([r.do_in[span, :]] * HEADS, axis=0) * heads_b for span in spans
            ]
            raws = [nt(grad, r.kv[s, :, width:]) for s, grad in zip(picks, grads)]
            slopes = []
            for s, span, raw in zip(picks, spans, raws):
                dots = r.dl[span, :]
                dots = jnp.concatenate([dots[:, h : h + 1] for h in range(HEADS)], axis=0)
                ds = half(wide(r.p[s]) * (raw - dots))
                r.ds[s] = ds
                slopes.append(ds)
            backs = [nn(ds, r.kv[s, :, :width]) for s, ds in zip(picks, slopes)]
            for span, dq in zip(spans, backs):
                dq = dq * r.heads[...]
                dq = sum(dq[h * H : h * H + H, :] for h in range(HEADS)) * 0.125
                r.dq_out[span, :] = half(dq)

    def cross_backward_pairs(b):
        unroll = 16

        @pl.loop(0, part_samples // unroll)
        def _(g):
            first = b * part_samples + g * unroll
            picks = [first + i for i in range(unroll)]
            spans = [pl.ds(pl.multiple_of(s * H, H), H) for s in picks]
            heads_b = r.heads_b[...]
            for pair in range(unroll // 2):
                keys, values = [], []
                for i in (2 * pair, 2 * pair + 1):
                    q = jnp.concatenate([r.qs[spans[i], :]] * HEADS, axis=0) * heads_b
                    grad = jnp.concatenate([r.do_in[spans[i], :]] * HEADS, axis=0) * heads_b
                    keys.append(tn(r.ds[picks[i]], q))
                    values.append(tn(r.p[picks[i]], grad))
                span = pl.ds(
                    pl.multiple_of(first * slots + pair * 2 * slots, 2 * slots), 2 * slots
                )
                r.dkv[span, :width] = half(jnp.concatenate(keys, axis=0))
                r.dkv[span, width:] = half(jnp.concatenate(values, axis=0))

    def send_query_grads(b):
        for k in range(1, n_cond):
            owner = lax.rem(c + k, n_cond)
            at = 4 * NB * n_cond + b * n_cond + k
            flights["dq", b, k] = send(
                r.dq_out.at[own_span(b, owner), :], r.dq_in.at[b, k], at, peer(k)
            )

    def self_backward(b):
        me = own_span(b, c)
        mine = pl.ds(b * own, own)
        total = wide(r.dq_out[me, :])
        for k in range(1, n_cond):
            flights["dq", b, k].wait_recv()
            total = total + wide(r.dq_in[b, k])
        dqc = half(total)
        r.dqc[mine, :] = dqc
        da2 = nt(dqc, w_cq())
        unit2, rate2 = unit_rows(r.x1[me, :])
        dx1 = r.dx2[mine, :] + unit_back(da2 * vec(2), unit2, rate2)
        dy1 = half(dx1)
        r.dy1[mine, :] = dy1
        do1 = half(nt(dy1, w_so()))
        causal = causal_mask()
        blocks = r.blocks[...]
        spans = [
            pl.ds(pl.multiple_of(b * part_rows + c * own + s * 64, 64), 64)
            for s in range(own // 64)
        ]
        q, k, v = (
            [r.qkv[span, i * width : (i + 1) * width] for span in spans] for i in range(3)
        )
        grads = [do1[s * 64 : s * 64 + 64, :] for s in range(own // 64)]
        v_blocks = [jnp.concatenate([x] * HEADS, axis=0) * blocks for x in v]
        dps = [nt(grad, vb) for grad, vb in zip(grads, v_blocks)]
        weights, k_blocks = self_weights(q, k, blocks, causal)
        pieces = []
        for i in range(own // 64):
            dv = tn(half(weights[i]), grads[i]) * wide(blocks)
            dots = spread(head_reduce(weights[i] * dps[i], "sum"))
            ds = half(weights[i] * (dps[i] - dots))
            dq = nn(ds, k_blocks[i]) * 0.125
            dk = tn(ds, q[i]) * wide(blocks)
            dk = sum(dk[h * 64 : h * 64 + 64, :] for h in range(HEADS)) * 0.125
            dv = sum(dv[h * 64 : h * 64 + 64, :] for h in range(HEADS))
            pieces.append(half(jnp.concatenate([dq, dk, dv], axis=1)))
        dqkv = jnp.concatenate(pieces, axis=0)
        r.dqkv[mine, :] = dqkv
        r.dx1[mine, :] = dx1
        add_vec(b, 2, column_sum(da2 * unit2))
        add_vec(b, 3, column_sum(da2))

    def self_backward_rest(b):
        me = own_span(b, c)
        mine = pl.ds(b * own, own)
        da1 = nt(r.dqkv[mine, :], w_qkv())
        unit1, rate1 = unit_rows(r.act[me, :])
        add_vec(b, 0, column_sum(da1 * unit1))
        add_vec(b, 1, column_sum(da1))
        r.ga16[me, :] = half(r.dx1[mine, :] + unit_back(da1 * vec(0), unit1, rate1))

    pair_first = 2 * hidden + 6 * width
    layout = {
        "up": (0, hidden),
        "down": (hidden, hidden),
        "row1": (2 * hidden, 2 * width),
        "row2": (2 * hidden + 2 * width, 2 * width),
        "row3": (2 * hidden + 4 * width, 2 * width),
        "pair": (pair_first, 2 * width),
    }
    set_at = {name: 5 * NB * n_cond + 10 * i for i, name in enumerate(layout)}
    vec_at = 5 * NB * n_cond + 10 * len(layout)
    share_at = vec_at + 5

    def owned(ref):
        return jnp.concatenate([ref[own_span(b, c), :] for b in range(NB)], axis=0)

    def up_grads():
        for j in range(hidden // width):
            here = slice(j * width, (j + 1) * width)
            r.g[here, :] = half(tn(r.a3[...], r.du[:, here]))

    def down_grads():
        for j in range(hidden // width):
            here = slice(j * width, (j + 1) * width)
            at = hidden + j * width
            r.g[at : at + width, :] = half(tn(r.hb[:, here], r.dz[...]))

    def put_row(j, values):
        first = 2 * hidden + j * width
        r.g[first : first + width, :] = half(values)

    def row1_grads():
        put_row(0, tn(r.o2[...], r.dy2[...]))
        put_row(1, tn(owned(r.a2), r.dqc[...]))

    def row2_grads():
        put_row(2, tn(owned(r.o1), r.dy1[...]))
        put_row(3, tn(owned(r.a1), r.dqkv[:, :width]))

    def row3_grads():
        for j in (1, 2):
            put_row(3 + j, tn(owned(r.a1), r.dqkv[:, j * width : (j + 1) * width]))

    def pair_grads(b):
        batch = 8
        step = batch * slots
        if b == 0:
            r.gw[...] = jnp.zeros_like(r.gw)

        @pl.loop(0, part_samples // batch)
        def _(g):
            span = pl.ds(pl.multiple_of((b * part_samples + g * batch) * slots, step), step)
            r.gw[...] += tn(r.mem[span, :], r.dkv[span, :])

        if b == NB - 1:
            for side in range(2):
                r.g[pair_first + side * width : pair_first + (side + 1) * width, :] = half(
                    r.gw[:, side * width : (side + 1) * width]
                )

    def set_sizes(name):
        first, count = layout[name]
        eighth = count // 8
        piece = max(16, eighth // n_line)
        return first, count // 2, eighth, piece, eighth // piece

    def at_rows(start, count):
        return pl.ds(pl.multiple_of(start, 16), count)

    def start(src, dst, at, to):
        pltpu.make_async_remote_copy(
            src_ref=src,
            dst_ref=dst,
            send_sem=r.ssem.at[at],
            recv_sem=r.rsem.at[at],
            device_id=to,
            device_id_type=MESH,
        ).start()

    def wait_rows(ref, count, at, which):
        view = ref.at[pl.ds(0, count), :]
        copy = pltpu.make_async_remote_copy(
            src_ref=view,
            dst_ref=view,
            send_sem=r.ssem.at[at],
            recv_sem=r.rsem.at[at],
            device_id=core_peer,
            device_id_type=MESH,
        )
        copy.wait_recv() if which == "recv" else copy.wait_send()

    def guard(full, cond, body):
        body() if full else pl.when(cond)(body)

    def wait_others(owners, piece, ref, at, which):
        if owners == n_line:
            wait_rows(ref, (n_line - 1) * piece, at, which)
        else:
            if owners > 1:
                pl.when(line < owners)(
                    lambda: wait_rows(ref, (owners - 1) * piece, at, which)
                )
            pl.when(line >= owners)(lambda: wait_rows(ref, owners * piece, at, which))

    def reduce_core(name):
        first, two, eighth, piece, owners = set_sizes(name)
        flights[name, 0] = send(
            r.g.at[at_rows(first + (1 - core) * two, two), :],
            r.rc.at[at_rows(first // 2, two), :],
            set_at[name],
            core_peer,
        )

    def reduce_plane(name):
        first, two, eighth, piece, owners = set_sizes(name)
        flights[name, 0].wait_recv()
        base = first // 2
        for k in (3, 1, 2, 0):
            span = at_rows(base + plane_place(k) * eighth, eighth)
            here = at_rows(first + core * two + plane_place(k) * eighth, eighth)
            r.rc[span, :] = half(wide(r.rc[span, :]) + wide(r.g[here, :]))
            if k:
                flights[name, k] = send(
                    r.rc.at[span, :],
                    r.rp.at[k - 1, pl.ds(first // 8, eighth), :],
                    set_at[name] + k,
                    plane_peer(k),
                )

    def reduce_line(name):
        first, two, eighth, piece, owners = set_sizes(name)
        total = wide(r.rc[at_rows(first // 2 + plane * eighth, eighth), :])
        base = first // 8
        for k in range(1, 4):
            flights[name, k].wait_recv()
            total = total + wide(r.rp[k - 1, base : base + eighth, :])
        r.ps[base : base + eighth, :] = half(total)
        for k in range(1, n_line):

            def go(k=k):
                start(
                    r.ps.at[at_rows(base + line_place(k) * piece, piece), :],
                    r.rz.at[pl.ds((layout_at(name) * n_line + k) * biggest, piece), :],
                    set_at[name] + 4,
                    line_peer(k),
                )

            guard(owners == n_line, line_place(k) < owners, go)

    biggest = max(set_sizes(name)[3] for name in layout)

    def layout_at(name):
        return list(layout).index(name)

    def own_eighth(name):
        first, two, eighth, piece, owners = set_sizes(name)
        return first + core * two + plane * eighth

    def gather_line(name):
        first, two, eighth, piece, owners = set_sizes(name)

        def finish():
            wait_rows(r.rz, (n_line - 1) * piece, set_at[name] + 4, "recv")
            total = wide(r.ps[at_rows(first // 8 + line * piece, piece), :])
            for k in range(1, n_line):
                at = (layout_at(name) * n_line + k) * biggest
                total = total + wide(r.rz[at : at + piece, :])
            here = at_rows(own_eighth(name) + line * piece, piece)
            r.tot[here, :] = half(total)
            for k in range(1, n_line):
                start(r.tot.at[here, :], r.tot.at[here, :], set_at[name] + 5, line_peer(k))

        guard(owners == n_line, line < owners, finish)

    def gather_plane(name):
        first, two, eighth, piece, owners = set_sizes(name)
        wait_others(owners, piece, r.tot, set_at[name] + 5, "recv")
        span = at_rows(own_eighth(name), eighth)
        for k in (3, 1, 2):
            flights[name, 5 + k] = send(
                r.tot.at[span, :], r.tot.at[span, :], set_at[name] + 5 + k, plane_peer(k)
            )

    def gather_core(name):
        first, two, eighth, piece, owners = set_sizes(name)
        for k in range(1, 4):
            flights[name, 5 + k].wait_recv()
        span = at_rows(first + core * two, two)
        flights[name, 9] = send(
            r.tot.at[span, :], r.tot.at[span, :], set_at[name] + 9, core_peer
        )

    def end_set(name):
        first, two, eighth, piece, owners = set_sizes(name)
        flights[name, 9].wait_recv()
        wait_others(owners, piece, r.ps, set_at[name] + 4, "send")
        guard(
            owners == n_line,
            line < owners,
            lambda: wait_rows(r.tot, (n_line - 1) * piece, set_at[name] + 5, "send"),
        )

    def small_core():
        r.v2[pl.ds(core, 1)] = r.vg[...][None]
        flights["v", 0] = send(r.v2.at[core], r.v2.at[core], vec_at, core_peer)

    def small_plane():
        flights["v", 0].wait_recv()
        r.v4[pl.ds(plane, 1)] = (r.v2[0] + r.v2[1])[None]
        for k in (3, 1, 2):
            flights["v", k] = send(
                r.v4.at[plane], r.v4.at[plane], vec_at + k, plane_peer(k)
            )

    def small_line():
        for k in range(1, 4):
            flights["v", k].wait_recv()
        r.vz[pl.ds(line, 1)] = (r.v4[0] + r.v4[1] + r.v4[2] + r.v4[3])[None]
        for k in range(1, n_line):
            start(r.vz.at[line], r.vz.at[line], vec_at + 4, line_peer(k))

    def small_wait(which):
        view = r.vz.at[pl.ds(0, n_line - 1)]
        copy = pltpu.make_async_remote_copy(
            src_ref=view,
            dst_ref=view,
            send_sem=r.ssem.at[vec_at + 4],
            recv_sem=r.rsem.at[vec_at + 4],
            device_id=core_peer,
            device_id_type=MESH,
        )
        copy.wait_recv() if which == "recv" else copy.wait_send()

    def small_end():
        small_wait("recv")
        total = r.vz[0]
        for k in range(1, n_line):
            total = total + r.vz[k]
        r.vtot[...] = total
        small_wait("send")

    def share(i, ref, b):
        at = share_at + 3 * (i * NB + b)
        span = own_span(b, c)
        flights["s", i, b, 0] = send(ref.at[span, :], ref.at[span, :], at, chip_peer)
        flights["s", i, b, 1] = send(ref.at[span, :], ref.at[span, :], at + 1, core_peer)

    def share_on(i, ref, b):
        at = share_at + 3 * (i * NB + b)
        flights["s", i, b, 0].wait_recv()
        span = own_span(b, lax.rem(c + 2, n_cond))
        flights["s", i, b, 2] = send(ref.at[span, :], ref.at[span, :], at + 2, core_peer)

    def share_end():
        for i in range(2):
            for b in range(NB):
                flights["s", i, b, 1].wait_recv()
                flights["s", i, b, 2].wait_recv()

    r.vg[11:16, :] = jnp.zeros((5, width), F32)
    loads["mw"].wait()
    r.mwb[...] = half(r.mw[...])
    loads["mem0"].wait()
    first = list(range(0, part_samples, 2))
    half_way = len(first) // 2
    for s in first[: half_way - 1]:
        pair_forward(s)
    for name in ("act", "vec", "rw"):
        loads[name].wait()
    r.rwb[:, : 4 * width] = half(r.rw[:, : 4 * width])
    pair_forward(first[half_way - 1])
    r.rwb[:, 4 * width :] = half(r.rw[:, 4 * width :])
    loads["mem1"].wait()
    first_forward(0, first[half_way:])
    load_moments()
    loads["mask"].wait()
    loads["flag"].wait()
    usable_rows()
    cross_forward(0)
    pl.semaphore_wait(barrier, len(friends))
    send_mixed(0)
    loads["mem2"].wait()
    loads["mem3"].wait()
    first_forward(1, list(range(part_samples, samples, 2)))
    cross_forward(1)
    send_mixed(1)
    loads["dw"].wait()
    r.dwb[...] = half(r.dw[...])
    loads["cot"].wait()
    middle(0)
    middle(1)
    up_grads()
    reduce_core("up")
    cross_backward(0)
    send_query_grads(0)
    down_grads()
    reduce_core("down")
    reduce_plane("up")
    cross_backward_pairs(0)
    cross_backward(1)
    send_query_grads(1)
    cross_backward_pairs(1)
    reduce_plane("down")
    pair_grads(0)
    pair_grads(1)
    reduce_core("pair")
    self_backward(0)
    share(0, r.out16, 0)
    self_backward(1)
    row3_grads()
    reduce_core("row3")
    reduce_line("down")
    row1_grads()
    reduce_core("row1")
    reduce_plane("pair")
    row2_grads()
    reduce_core("row2")
    self_backward_rest(0)
    self_backward_rest(1)
    small_core()
    reduce_plane("row3")
    reduce_line("up")
    reduce_plane("row2")
    gather_line("down")
    reduce_line("row3")
    reduce_plane("row1")
    small_plane()
    gather_line("up")
    reduce_line("pair")
    share(1, r.ga16, 1)
    share(1, r.ga16, 0)
    gather_plane("down")
    share(0, r.out16, 1)
    reduce_line("row1")
    gather_line("row3")
    reduce_line("row2")
    small_line()
    share_on(0, r.out16, 0)
    gather_line("pair")
    gather_plane("up")
    gather_line("row1")
    gather_core("down")
    gather_plane("row3")
    share_on(1, r.ga16, 0)
    gather_line("row2")
    gather_plane("pair")
    gather_core("up")
    gather_plane("row1")
    share_on(0, r.out16, 1)
    gather_plane("row2")
    gather_core("row3")
    gather_core("pair")
    share_on(1, r.ga16, 1)
    gather_core("row1")
    gather_core("row2")
    small_end()
    share_end()
    for name in ("m_r", "m_d", "m_p", "a_r", "a_d", "a_p"):
        loads[name].wait()
    for name in layout:
        end_set(name)
    for copy in pending:
        copy.wait_send()


def step_kernel(names, token_count, *refs):
    r = Names()
    for name, ref in zip(names, refs, strict=True):
        setattr(r, name, ref)
    width = r.w_p.shape[0]
    hidden = r.w_d.shape[0]
    keep = 1.0 - (1.0 + STEP) ** (-0.75)
    copies = []

    def store(src, dst):
        copy = pltpu.make_async_copy(src, dst, r.sem.at[len(copies)])
        copy.start()
        copies.append(copy)

    def update(weight, grad, moment, average):
        scaled = grad / token_count
        moment_new = INERTIA * moment + scaled
        weight_new = weight - STEP_RATE * (scaled + INERTIA * moment_new)
        average_new = keep * average + (1.0 - keep) * weight_new
        return moment_new, weight_new, average_new

    def renew(prefix, row, column, first):
        rows = 32
        cols = slice(column, column + width)

        @pl.loop(0, width // rows, unroll=8)
        def _(i):
            at = pl.multiple_of(i * rows, rows)
            grad = wide(r.tot[pl.ds(first + at, rows), :])
            here = pl.ds(row + at, rows)
            old = [getattr(r, kind + "_" + prefix)[here, cols] for kind in "wma"]
            new = update(old[0], grad, old[1], old[2])
            for kind, value in zip("mwa", new):
                getattr(r, prefix + kind)[here, cols] = value

        for kind in "mwa":
            view = (slice(row, row + width), cols)
            store(getattr(r, prefix + kind).at[view], getattr(r, prefix + kind + "_h").at[view])

    pair_first = 2 * hidden + 6 * width
    order = {5: 0, 4: 1, 3: 2, 0: 3, 1: 4, 2: 5}
    blocks = [("d", j * width, 0, hidden + j * width) for j in range(hidden // width)]
    blocks += [("r", 0, (6 + j) * width, j * width) for j in range(hidden // width)]
    blocks += [("r", 0, j * width, 2 * hidden + order[j] * width) for j in range(6)]
    blocks += [("p", 0, j * width, pair_first + j * width) for j in range(2)]

    r.mwb[...] = half(r.w_p[...])
    total_rows = r.dkv.shape[0]
    chunks = 8
    step = total_rows // chunks
    for i in range(chunks):
        for block in blocks[i * len(blocks) // chunks : (i + 1) * len(blocks) // chunks]:
            renew(*block)
        span = pl.ds(i * step, step)
        r.gm[span, :] = nt(r.dkv[span, :], r.mwb[...])
        store(r.gm.at[span, :], r.gm_h.at[span, :])
    r.out[...] = wide(r.out16[...])
    store(r.out, r.out_h)
    r.ga[...] = wide(r.ga16[...])
    store(r.ga, r.ga_h)
    new = update(r.w_v[...], r.vtot[: r.w_v.shape[0], :], r.m_v[...], r.a_v[...])
    for kind, value in zip("mwa", new):
        getattr(r, "v" + kind)[...] = value
        store(getattr(r, "v" + kind), getattr(r, "v" + kind + "_h"))
    for copy in copies:
        copy.wait()


def per_device(
    actions,
    memory,
    patch_flags,
    memory_mask,
    cotangent,
    row_weights,
    memory_weights,
    down_weight,
    vectors,
    row_momentum,
    memory_momentum,
    down_momentum,
    vector_momentum,
    row_average,
    memory_average,
    down_average,
    vector_average,
):
    rows, width = actions.shape
    samples = rows // H
    slots = memory.shape[1]
    hidden = down_weight.shape[0]
    n_cond = lax.axis_size("cond")
    n_dp = lax.axis_size("dp")
    part_rows = rows // NB
    own = part_rows // n_cond
    total = 2 * hidden + 8 * width
    flat = samples * slots
    ins = {
        "act_h": actions,
        "mem_h": memory.reshape(flat, width),
        "mask_h": memory_mask,
        "flag_h": patch_flags.reshape(1, samples),
        "cot_h": cotangent,
        "rw_h": row_weights,
        "mw_h": memory_weights,
        "dw_h": down_weight,
        "vec_h": vectors,
        "m_r_h": row_momentum,
        "m_d_h": down_momentum,
        "m_p_h": memory_momentum,
        "a_r_h": row_average,
        "a_d_h": down_average,
        "a_p_h": memory_average,
    }
    outs = {
        "tot": ((total, width), BF),
        "vtot": ((16, width), F32),
        "dkv": ((flat, 2 * width), BF),
        "out16": ((rows, width), BF),
        "ga16": ((rows, width), BF),
        "rw": (row_weights.shape, F32),
        "dw": (down_weight.shape, F32),
        "mw": (memory_weights.shape, F32),
        "m_r": (row_weights.shape, F32),
        "m_d": (down_weight.shape, F32),
        "m_p": (memory_weights.shape, F32),
        "a_r": (row_weights.shape, F32),
        "a_d": (down_weight.shape, F32),
        "a_p": (memory_weights.shape, F32),
    }

    n_line = n_dp // 2
    biggest = max(16, hidden // 8 // n_line)

    scratch = {
        "act": ((rows, width), F32),
        "vec": (vectors.shape, F32),
        "mem": ((flat, width), BF),
        "mask": (memory_mask.shape, jnp.int32),
        "flag": ((1, samples), jnp.int32),
        "cot": ((rows, width), F32),
        "rwb": (row_weights.shape, BF),
        "mwb": (memory_weights.shape, BF),
        "dwb": (down_weight.shape, BF),
        "blocks": ((256, 256), BF),
        "heads": ((64, 256), F32),
        "heads_b": ((64, 256), BF),
        "a1": ((rows, width), BF),
        "qkv": ((rows, 3 * width), BF),
        "o1": ((rows, width), BF),
        "x1": ((rows, width), F32),
        "a2": ((rows, width), BF),
        "qs": ((rows, width), BF),
        "kv": ((samples, slots, 2 * width), BF),
        "use": ((samples, slots), F32),
        "p": ((samples, 64, slots), BF),
        "ds": ((samples, 64, slots), BF),
        "o_out": ((rows, width), BF),
        "top": ((rows, 128), F32),
        "total": ((rows, 128), F32),
        "st_in": ((NB, n_cond, 16, 128), F32),
        "st_out": ((NB, n_cond, 16, 128), F32),
        "o_in": ((NB, n_cond, own, width), BF),
        "o2": ((NB * own, width), BF),
        "a3": ((NB * own, width), BF),
        "dz": ((NB * own, width), BF),
        "hb": ((NB * own, hidden), BF),
        "du": ((NB * own, hidden), BF),
        "dx2": ((NB * own, width), F32),
        "dx1": ((NB * own, width), F32),
        "dy2": ((NB * own, width), BF),
        "dqc": ((NB * own, width), BF),
        "dy1": ((NB * own, width), BF),
        "dqkv": ((NB * own, 3 * width), BF),
        "do_in": ((rows, width), BF),
        "do_out": ((NB, n_cond, own, width), BF),
        "dl_in": ((NB, n_cond, 8, 128), F32),
        "dl_out": ((NB, n_cond, 8, 128), F32),
        "dl": ((rows, 128), F32),
        "dq_out": ((rows, width), BF),
        "dq_in": ((NB, n_cond, own, width), BF),
        "vg": ((16, width), F32),
        "v2": ((2, 16, width), F32),
        "v4": ((4, 16, width), F32),
        "vz": ((n_line, 16, width), F32),
        "g": ((total, width), BF),
        "gw": ((width, 2 * width), F32),
        "rc": ((total // 2, width), BF),
        "rp": ((3, total // 8, width), BF),
        "ps": ((total // 8, width), BF),
        "rz": ((6 * n_line * biggest, width), BF),
    }
    sems = {
        "load_sem": pltpu.SemaphoreType.DMA((24,)),
        "ssem": pltpu.SemaphoreType.DMA((128,)),
        "rsem": pltpu.SemaphoreType.DMA((128,)),
    }
    whole = pl.BlockSpec(memory_space=pltpu.VMEM)
    far = pl.BlockSpec(memory_space=pltpu.HBM)
    names = list(ins) + list(outs) + list(scratch) + list(sems)
    sizes = (rows, samples, slots, n_cond, n_dp, width)
    made = pl.pallas_call(
        functools.partial(layer_kernel, names, sizes),
        out_shape=[pltpu.VMEM(*v) for v in outs.values()],
        in_specs=[far] * len(ins),
        out_specs=[whole] * len(outs),
        scratch_shapes=[pltpu.VMEM(*v) for v in scratch.values()] + list(sems.values()),
        compiler_params=pltpu.CompilerParams(
            collective_id=0, has_side_effects=True, vmem_limit_bytes=32 * MIB
        ),
        name="layer",
    )(*(pltpu.with_memory_space_constraint(v, pltpu.HBM) for v in ins.values()))

    ins2 = dict(zip(outs, made, strict=True))
    ins2 |= {"w_v": vectors, "m_v": vector_momentum, "a_v": vector_average}
    outs2 = {
        "out": (rows, width),
        "ga": (rows, width),
        "gm": (flat, width),
    }
    for prefix, array in (("r", row_weights), ("p", memory_weights), ("d", down_weight), ("v", vectors)):
        for kind in "mwa":
            outs2[prefix + kind] = array.shape
    renamed = {"rw": "w_r", "dw": "w_d", "mw": "w_p"}
    names2 = [renamed.get(k, k) for k in ins2]
    names2 += [k + "_h" for k in outs2] + list(outs2) + ["mwb", "sem"]
    results = pl.pallas_call(
        functools.partial(step_kernel, names2, float(rows * n_dp)),
        out_shape=[jax.ShapeDtypeStruct(v, F32) for v in outs2.values()],
        in_specs=[whole] * len(ins2),
        out_specs=[far] * len(outs2),
        scratch_shapes=[pltpu.VMEM(v, F32) for v in outs2.values()]
        + [pltpu.VMEM(memory_weights.shape, BF), pltpu.SemaphoreType.DMA((64,))],
        compiler_params=pltpu.CompilerParams(vmem_limit_bytes=26 * MIB),
        name="step",
    )(*ins2.values())
    out, ga, gm = results[:3]
    return (out, ga, gm.reshape(samples, slots, width), *results[3:])


def solution(mesh):
    in_specs = (
        P("dp", None),
        P("dp", "cond", None),
        P("dp", "cond"),
        P("dp", "cond"),
        P("dp", None),
    ) + (P(),) * 12
    out_specs = (P("dp", None), P("dp", None), P("dp", "cond", None)) + (P(),) * 12
    return jax.shard_map(
        per_device, mesh=mesh, in_specs=in_specs, out_specs=out_specs, check_vma=False
    )
```

```python
import functools
import math

import jax
import jax.numpy as jnp
from jax import lax
from jax.experimental import pallas as pl
from jax.experimental.pallas import tpu as pltpu
from jax.sharding import PartitionSpec as P

HEADS = 4
H = 16
PATCHES = 196
STEP = 10
INERTIA = 0.9
STEP_RATE = 1.0
LOWEST = -1e30
NB = 2
MESH = pl.DeviceIdType.MESH
MIB = 2**20
BF = jnp.bfloat16
F32 = jnp.float32


def half(values):
    return values.astype(BF)


def wide(values):
    return values.astype(F32)


def nn(a, b):
    return jnp.dot(a, b, preferred_element_type=F32)


def nt(a, b):
    return lax.dot_general(a, b, (((1,), (1,)), ((), ())), preferred_element_type=F32)


def tn(a, b):
    return lax.dot_general(a, b, (((0,), (0,)), ((), ())), preferred_element_type=F32)


def unit_rows(values):
    centered = values - jnp.mean(values, axis=-1, keepdims=True)
    rate = lax.rsqrt(jnp.mean(centered * centered, axis=-1, keepdims=True) + 1e-05)
    return centered * rate, rate


def unit_back(grad, unit, rate):
    return rate * (
        grad
        - jnp.mean(grad, axis=-1, keepdims=True)
        - unit * jnp.mean(grad * unit, axis=-1, keepdims=True)
    )


def column_sum(values):
    return jnp.sum(values, axis=0, keepdims=True)


def head_columns(table, first):
    rows = table.shape[0]
    low_lane = lax.broadcasted_iota(jnp.int32, (rows, 128), 1) < 64
    cols = [table[:, first + h : first + h + 1] for h in range(HEADS)]
    return jnp.concatenate(
        [jnp.where(low_lane, cols[0], cols[1]), jnp.where(low_lane, cols[2], cols[3])], axis=1
    )


def head_reduce(values, kind):
    rows = values.shape[0]
    low_lane = lax.broadcasted_iota(jnp.int32, (rows, 128), 1) < 64
    fill = LOWEST if kind == "max" else 0.0
    cols = []
    for pair in range(2):
        part = values[:, pair * 128 : pair * 128 + 128]
        for keep_low in (True, False):
            picked = jnp.where(low_lane == keep_low, part, fill)
            if kind == "max":
                cols.append(jnp.max(picked, axis=1, keepdims=True))
            else:
                cols.append(jnp.sum(picked, axis=1, keepdims=True))
    return cols


def spread(cols):
    rows = cols[0].shape[0]
    low_lane = lax.broadcasted_iota(jnp.int32, (rows, 128), 1) < 64
    return jnp.concatenate(
        [jnp.where(low_lane, cols[0], cols[1]), jnp.where(low_lane, cols[2], cols[3])], axis=1
    )


def lanes_of(cols):
    rows = cols[0].shape[0]
    lane = lax.broadcasted_iota(jnp.int32, (rows, 128), 1)
    table = jnp.zeros((rows, 128), F32)
    for h, col in enumerate(cols):
        table = jnp.where(lane == h, col, table)
    return table


def pad_rows(values, rows):
    missing = rows - values.shape[0]
    if missing == 0:
        return values
    return jnp.concatenate([values, jnp.zeros((missing, values.shape[1]), values.dtype)], axis=0)


def self_weights(queries, keys, blocks, causal, beside=lambda: None):
    k_blocks = [jnp.concatenate([k] * HEADS, axis=0) * blocks for k in keys]
    scores = [nt(q, kb) for q, kb in zip(queries, k_blocks)]
    beside()
    weights = []
    for score in scores:
        score = jnp.where(causal, score * 0.125, LOWEST)
        top = spread(head_reduce(score, "max"))
        raised = jnp.where(causal, jnp.exp(score - top), 0.0)
        weights.append(raised / spread(head_reduce(raised, "sum")))
    return weights, k_blocks


class Names:
    pass


def layer_kernel(names, sizes, *refs):
    r = Names()
    for name, ref in zip(names, refs, strict=True):
        setattr(r, name, ref)
    rows, samples, slots, n_cond, n_dp, width = sizes
    hidden = r.dw.shape[0]
    part_rows = rows // NB
    own = part_rows // n_cond
    part_samples = samples // NB
    c = lax.axis_index("cond")
    d = lax.axis_index("dp")

    def peer(k):
        return (d, lax.rem(c + k, n_cond))

    core = lax.rem(c, 2)
    side_x = lax.rem(d, 2)
    side_y = c // 2
    plane = 2 * side_x + side_y
    line = d // 2
    n_line = n_dp // 2
    core_peer = (d, c + 1 - 2 * core)
    chip_peer = (d, lax.rem(c + 2, n_cond))

    def plane_place(k):
        x = 1 - side_x if k & 1 else side_x
        y = 1 - side_y if k & 2 else side_y
        return 2 * x + y

    def plane_peer(k):
        return (
            d + 1 - 2 * side_x if k & 1 else d,
            lax.rem(c + 2, n_cond) if k & 2 else c,
        )

    def line_place(k):
        return lax.rem(line + k, n_line)

    def line_peer(k):
        return (2 * line_place(k) + side_x, c)

    barrier = pltpu.get_barrier_semaphore()
    friends = [peer(k) for k in range(1, n_cond)]
    friends += [plane_peer(k) for k in (1, 3)]
    friends += [line_peer(k) for k in range(1, n_line)]
    for friend in friends:
        pl.semaphore_signal(barrier, inc=1, device_id=friend, device_id_type=MESH)

    loads = {}

    def load(name, src, dst, at):
        copy = pltpu.make_async_copy(src, dst, r.load_sem.at[at])
        copy.start()
        loads[name] = copy

    mem_parts = 4
    mem_rows = samples * slots // mem_parts

    def load_memory(i):
        span = pl.ds(i * mem_rows, mem_rows)
        load(f"mem{i}", r.mem_h.at[span], r.mem.at[span], 8 + i)

    load("mw", r.mw_h, r.mw, 3)
    load_memory(0)
    load("act", r.act_h, r.act, 0)
    load("vec", r.vec_h, r.vec, 2)
    load("rw", r.rw_h, r.rw, 1)
    load_memory(1)
    load("mask", r.mask_h, r.mask, 4)
    load("flag", r.flag_h, r.flag, 5)
    load("dw", r.dw_h, r.dw, 6)
    load("cot", r.cot_h, r.cot, 7)
    load_memory(2)
    load_memory(3)

    def load_moments():
        for i, name in enumerate(("m_r", "m_d", "m_p", "a_r", "a_d", "a_p")):
            load(name, getattr(r, name + "_h"), getattr(r, name), 16 + i)

    lane256 = lax.broadcasted_iota(jnp.int32, (256, 256), 1)
    row256 = lax.broadcasted_iota(jnp.int32, (256, 256), 0)
    r.blocks[...] = half(jnp.where(lane256 // 64 == row256 // 64, 1.0, 0.0))
    lane64 = lax.broadcasted_iota(jnp.int32, (64, 256), 1)
    row64 = lax.broadcasted_iota(jnp.int32, (64, 256), 0)
    r.heads[...] = jnp.where(lane64 // 64 == row64 // 16, 1.0, 0.0)
    r.heads_b[...] = half(r.heads[...])

    def causal_mask():
        key = lax.rem(lane64, 64)
        return (key // H == row64 // H) & (key <= row64)

    def vec(i):
        return r.vec[i : i + 1, :]

    w_qkv = lambda: r.rwb[:, : 3 * width]
    w_so = lambda: r.rwb[:, 3 * width : 4 * width]
    w_cq = lambda: r.rwb[:, 4 * width : 5 * width]
    w_co = lambda: r.rwb[:, 5 * width : 6 * width]
    w_up = lambda: r.rwb[:, 6 * width :]

    def pair_forward(first):
        span = pl.ds(pl.multiple_of(first * slots, 2 * slots), 2 * slots)
        kv = nn(r.mem[span, :], r.mwb[...])
        for s in range(2):
            r.kv[first + s] = half(kv[s * slots : (s + 1) * slots, :])

    def first_forward(b, waiting):
        def fill(count):
            for _ in range(min(count, len(waiting))):
                pair_forward(waiting.pop(0))

        span = pl.ds(b * part_rows, part_rows)
        x = r.act[span, :]
        unit, _ = unit_rows(x)
        a1 = half(unit * vec(0) + vec(1))
        r.a1[span, :] = a1
        fill(1)
        qkv = half(nn(a1, w_qkv()))
        r.qkv[span, :] = qkv
        fill(1)
        causal = causal_mask()
        blocks = r.blocks[...]
        pieces = [qkv[s * 64 : s * 64 + 64, :] for s in range(part_rows // 64)]
        q, k, v = ([p[:, i * width : (i + 1) * width] for p in pieces] for i in range(3))
        v_blocks = [jnp.concatenate([x] * HEADS, axis=0) * blocks for x in v]
        weights, _ = self_weights(q, k, blocks, causal, lambda: fill(2))
        mixed = [nn(half(w), vb) for w, vb in zip(weights, v_blocks)]
        o1 = half(jnp.concatenate(mixed, axis=0))
        r.o1[span, :] = o1
        fill(1)
        x1 = x + nn(o1, w_so())
        r.x1[span, :] = x1
        fill(2)
        unit2, _ = unit_rows(x1)
        a2 = half(unit2 * vec(2) + vec(3))
        r.a2[span, :] = a2
        r.qs[span, :] = half(nn(a2, w_cq()) * 0.125)
        fill(len(waiting))

    def usable_rows():
        position = lax.broadcasted_iota(jnp.int32, (samples, slots), 1)
        square = (samples, samples)
        diagonal = lax.broadcasted_iota(jnp.int32, square, 0) == lax.broadcasted_iota(
            jnp.int32, square, 1
        )
        counts = jnp.where(diagonal, jnp.broadcast_to(r.flag[...], square), 0)
        counts = jnp.sum(counts.astype(F32), axis=1, keepdims=True)
        kept = (position.astype(F32) < counts) & (r.mask[...] == 1)
        time_token = (position == PATCHES) & (c == 0)
        r.use[...] = jnp.where(kept | time_token, 1.0, 0.0)

    def cross_forward(b):
        unroll = 16

        @pl.loop(0, part_samples // unroll)
        def _(g):
            picks = [b * part_samples + g * unroll + i for i in range(unroll)]
            spans = [pl.ds(pl.multiple_of(s * H, H), H) for s in picks]
            heads_b = r.heads_b[...]
            scores = []
            for s, span in zip(picks, spans):
                q = jnp.concatenate([r.qs[span, :]] * HEADS, axis=0) * heads_b
                scores.append(nt(q, r.kv[s, :, :width]))
            weights = []
            for s, span, score in zip(picks, spans, scores):
                usable = jnp.broadcast_to(r.use[pl.ds(s, 1), :], (64, slots)) > 0.5
                score = jnp.where(usable, score, LOWEST)
                top = jnp.max(score, axis=1, keepdims=True)
                raised = jnp.where(usable, jnp.exp(score - top), 0.0)
                total = jnp.sum(raised, axis=1, keepdims=True)
                p = half(raised)
                r.p[s] = p
                weights.append(p)
                r.top[span, :] = lanes_of([top[h * H : h * H + H, :] for h in range(HEADS)])
                r.total[span, :] = lanes_of([total[h * H : h * H + H, :] for h in range(HEADS)])
            mixes = [nn(p, r.kv[s, :, width:]) for s, p in zip(picks, weights)]
            for span, mixed in zip(spans, mixes):
                mixed = mixed * r.heads[...]
                r.o_out[span, :] = half(sum(mixed[h * H : h * H + H, :] for h in range(HEADS)))

    pending = []

    def send(src, dst, at, to):
        copy = pltpu.make_async_remote_copy(
            src_ref=src,
            dst_ref=dst,
            send_sem=r.ssem.at[at],
            recv_sem=r.rsem.at[at],
            device_id=to,
            device_id_type=MESH,
        )
        copy.start()
        pending.append(copy)
        return copy

    def own_span(b, owner):
        return pl.ds(pl.multiple_of(b * part_rows + owner * own, own), own)

    flights = {}

    def send_mixed(b):
        for k in range(n_cond):
            owner = lax.rem(c + k, n_cond)
            span = own_span(b, owner)
            stats = jnp.concatenate(
                [
                    pad_rows(r.top[span, :], 128).T[:8, :],
                    pad_rows(r.total[span, :], 128).T[:8, :],
                ],
                axis=0,
            )
            if k == 0:
                r.st_in[b, 0] = stats
                r.o_in[b, 0] = r.o_out[span, :]
            else:
                r.st_out[b, k] = stats
                at = (b * n_cond + k) * 2
                flights["o", b, k] = (
                    send(r.st_out.at[b, k], r.st_in.at[b, k], at, peer(k)),
                    send(r.o_out.at[span, :], r.o_in.at[b, k], at + 1, peer(k)),
                )

    def middle(b):
        mine = pl.ds(b * own, own)
        me = own_span(b, c)
        biases = hidden // width
        cot = r.cot[me, :]
        dz = half(cot)
        r.dz[mine, :] = dz
        grad_acts = [nt(dz, r.dwb[j * width : (j + 1) * width, :]) for j in range(biases)]
        for k in range(1, n_cond):
            for copy in flights["o", b, k]:
                copy.wait_recv()
        tops = [r.st_in[b, k, :8, :] for k in range(n_cond)]
        top = functools.reduce(jnp.maximum, tops)
        raised = [jnp.exp(t - top) for t in tops]
        total = sum(w * r.st_in[b, k, 8:, :] for k, w in enumerate(raised))
        total = jnp.maximum(total, 0.5)
        shares = [w / total for w in raised]
        table = pad_rows(jnp.concatenate(shares, axis=0), 128).T[:own, :]
        spreads = [head_columns(table, 8 * k) for k in range(n_cond)]
        o2 = sum(spreads[k] * wide(r.o_in[b, k]) for k in range(n_cond))
        o2b = half(o2)
        r.o2[mine, :] = o2b
        x2 = r.x1[me, :] + nn(o2b, w_co())
        unit, rate = unit_rows(x2)
        a3 = half(unit * vec(4) + vec(5))
        r.a3[mine, :] = a3
        ups = [slice(6 * width + j * width, 6 * width + (j + 1) * width) for j in range(biases)]
        downs = [slice(j * width, (j + 1) * width) for j in range(biases)]
        us = [nn(a3, r.rwb[:, cols]) for cols in ups]
        acts, slopes = [], []
        for j in range(biases):
            u = us[j] + vec(6 + j)
            below = 0.5 + 0.5 * lax.erf(u * (2.0**-0.5))
            acts.append(half(u * below))
            slopes.append(
                below + u * (jnp.exp(-0.5 * u * u) * (1.0 / math.sqrt(2.0 * math.pi)))
            )
        dus = []
        for j in range(biases):
            du = half(grad_acts[j] * slopes[j])
            r.du[mine, downs[j]] = du
            dus.append(du)
        da3 = sum(nt(du, r.rwb[:, cols]) for du, cols in zip(dus, ups))
        dx2 = cot + unit_back(da3 * vec(4), unit, rate)
        r.dx2[mine, :] = dx2
        dy = half(dx2)
        r.dy2[mine, :] = dy
        do2 = wide(half(nt(dy, w_co())))
        delta = lanes_of(head_reduce(do2 * wide(o2b), "sum"))
        delta = pad_rows(delta, 128).T[:8, :]
        for k in range(n_cond):
            grads = half(do2 * spreads[k])
            dots = delta * shares[k]
            if k == 0:
                r.do_in[me, :] = grads
                r.dl_in[b, 0] = dots
            else:
                r.do_out[b, k] = grads
                r.dl_out[b, k] = dots
                at = (NB * n_cond + b * n_cond + k) * 2
                to = peer(n_cond - k)
                flights["do", b, k] = (
                    send(r.dl_out.at[b, k], r.dl_in.at[b, k], at, to),
                    send(r.do_out.at[b, k], r.do_in.at[me, :], at + 1, to),
                )
        for j in range(biases):
            r.hb[mine, downs[j]] = acts[j]
            add_vec(b, 6 + j, column_sum(wide(dus[j])))
        out = x2 + vec(6 + biases)
        out = out + sum(nn(hb, r.dwb[here, :]) for hb, here in zip(acts, downs))
        r.out16[me, :] = half(out)
        add_vec(b, 6 + biases, column_sum(wide(dz)))
        add_vec(b, 4, column_sum(da3 * unit))
        add_vec(b, 5, column_sum(da3))

    def add_vec(b, i, values):
        if b == 0:
            r.vg[i : i + 1, :] = values
        else:
            r.vg[i : i + 1, :] += values

    def cross_backward(b):
        for k in range(n_cond):
            owner = lax.rem(c + k, n_cond)
            if k:
                for copy in flights["do", b, k]:
                    copy.wait_recv()
            r.dl[own_span(b, owner), :] = pad_rows(r.dl_in[b, k], 128).T[:own, :]
        unroll = 16

        @pl.loop(0, part_samples // unroll)
        def _(g):
            first = b * part_samples + g * unroll
            picks = [first + i for i in range(unroll)]
            spans = [pl.ds(pl.multiple_of(s * H, H), H) for s in picks]
            heads_b = r.heads_b[...]
            grads = [
                jnp.concatenate([r.do_in[span, :]] * HEADS, axis=0) * heads_b for span in spans
            ]
            raws = [nt(grad, r.kv[s, :, width:]) for s, grad in zip(picks, grads)]
            slopes = []
            for s, span, raw in zip(picks, spans, raws):
                dots = r.dl[span, :]
                dots = jnp.concatenate([dots[:, h : h + 1] for h in range(HEADS)], axis=0)
                ds = half(wide(r.p[s]) * (raw - dots))
                r.ds[s] = ds
                slopes.append(ds)
            backs = [nn(ds, r.kv[s, :, :width]) for s, ds in zip(picks, slopes)]
            for span, dq in zip(spans, backs):
                dq = dq * r.heads[...]
                dq = sum(dq[h * H : h * H + H, :] for h in range(HEADS)) * 0.125
                r.dq_out[span, :] = half(dq)

    def cross_backward_pairs(b):
        unroll = 16

        @pl.loop(0, part_samples // unroll)
        def _(g):
            first = b * part_samples + g * unroll
            picks = [first + i for i in range(unroll)]
            spans = [pl.ds(pl.multiple_of(s * H, H), H) for s in picks]
            heads_b = r.heads_b[...]
            for pair in range(unroll // 2):
                keys, values = [], []
                for i in (2 * pair, 2 * pair + 1):
                    q = jnp.concatenate([r.qs[spans[i], :]] * HEADS, axis=0) * heads_b
                    grad = jnp.concatenate([r.do_in[spans[i], :]] * HEADS, axis=0) * heads_b
                    keys.append(tn(r.ds[picks[i]], q))
                    values.append(tn(r.p[picks[i]], grad))
                span = pl.ds(
                    pl.multiple_of(first * slots + pair * 2 * slots, 2 * slots), 2 * slots
                )
                r.dkv[span, :width] = half(jnp.concatenate(keys, axis=0))
                r.dkv[span, width:] = half(jnp.concatenate(values, axis=0))

    def send_query_grads(b):
        for k in range(1, n_cond):
            owner = lax.rem(c + k, n_cond)
            at = 4 * NB * n_cond + b * n_cond + k
            flights["dq", b, k] = send(
                r.dq_out.at[own_span(b, owner), :], r.dq_in.at[b, k], at, peer(k)
            )

    def self_backward(b):
        me = own_span(b, c)
        mine = pl.ds(b * own, own)
        total = wide(r.dq_out[me, :])
        for k in range(1, n_cond):
            flights["dq", b, k].wait_recv()
            total = total + wide(r.dq_in[b, k])
        dqc = half(total)
        r.dqc[mine, :] = dqc
        da2 = nt(dqc, w_cq())
        unit2, rate2 = unit_rows(r.x1[me, :])
        dx1 = r.dx2[mine, :] + unit_back(da2 * vec(2), unit2, rate2)
        dy1 = half(dx1)
        r.dy1[mine, :] = dy1
        do1 = half(nt(dy1, w_so()))
        causal = causal_mask()
        blocks = r.blocks[...]
        spans = [
            pl.ds(pl.multiple_of(b * part_rows + c * own + s * 64, 64), 64)
            for s in range(own // 64)
        ]
        q, k, v = (
            [r.qkv[span, i * width : (i + 1) * width] for span in spans] for i in range(3)
        )
        grads = [do1[s * 64 : s * 64 + 64, :] for s in range(own // 64)]
        v_blocks = [jnp.concatenate([x] * HEADS, axis=0) * blocks for x in v]
        dps = [nt(grad, vb) for grad, vb in zip(grads, v_blocks)]
        weights, k_blocks = self_weights(q, k, blocks, causal)
        pieces = []
        for i in range(own // 64):
            dv = tn(half(weights[i]), grads[i]) * wide(blocks)
            dots = spread(head_reduce(weights[i] * dps[i], "sum"))
            ds = half(weights[i] * (dps[i] - dots))
            dq = nn(ds, k_blocks[i]) * 0.125
            dk = tn(ds, q[i]) * wide(blocks)
            dk = sum(dk[h * 64 : h * 64 + 64, :] for h in range(HEADS)) * 0.125
            dv = sum(dv[h * 64 : h * 64 + 64, :] for h in range(HEADS))
            pieces.append(half(jnp.concatenate([dq, dk, dv], axis=1)))
        dqkv = jnp.concatenate(pieces, axis=0)
        r.dqkv[mine, :] = dqkv
        r.dx1[mine, :] = dx1
        add_vec(b, 2, column_sum(da2 * unit2))
        add_vec(b, 3, column_sum(da2))

    def self_backward_rest(b):
        me = own_span(b, c)
        mine = pl.ds(b * own, own)
        da1 = nt(r.dqkv[mine, :], w_qkv())
        unit1, rate1 = unit_rows(r.act[me, :])
        add_vec(b, 0, column_sum(da1 * unit1))
        add_vec(b, 1, column_sum(da1))
        r.ga16[me, :] = half(r.dx1[mine, :] + unit_back(da1 * vec(0), unit1, rate1))

    pair_first = 2 * hidden + 6 * width
    layout = {
        "up": (0, hidden),
        "down": (hidden, hidden),
        "row1": (2 * hidden, 2 * width),
        "row2": (2 * hidden + 2 * width, 4 * width),
        "pair": (pair_first, 2 * width),
    }
    set_at = {name: 5 * NB * n_cond + 10 * i for i, name in enumerate(layout)}
    vec_at = 5 * NB * n_cond + 10 * len(layout)
    share_at = vec_at + 5

    def owned(ref):
        return jnp.concatenate([ref[own_span(b, c), :] for b in range(NB)], axis=0)

    def up_grads():
        for j in range(hidden // width):
            here = slice(j * width, (j + 1) * width)
            r.g[here, :] = half(tn(r.a3[...], r.du[:, here]))

    def down_grads():
        for j in range(hidden // width):
            here = slice(j * width, (j + 1) * width)
            at = hidden + j * width
            r.g[at : at + width, :] = half(tn(r.hb[:, here], r.dz[...]))

    def put_row(j, values):
        first = 2 * hidden + j * width
        r.g[first : first + width, :] = half(values)

    def row1_grads():
        put_row(0, tn(r.o2[...], r.dy2[...]))
        put_row(1, tn(owned(r.a2), r.dqc[...]))

    def row2_grads():
        put_row(2, tn(owned(r.o1), r.dy1[...]))
        put_row(3, tn(owned(r.a1), r.dqkv[:, :width]))

    def row3_grads():
        for j in (1, 2):
            put_row(3 + j, tn(owned(r.a1), r.dqkv[:, j * width : (j + 1) * width]))

    def pair_grads(b):
        batch = 8
        step = batch * slots
        if b == 0:
            r.gw[...] = jnp.zeros_like(r.gw)

        @pl.loop(0, part_samples // batch)
        def _(g):
            span = pl.ds(pl.multiple_of((b * part_samples + g * batch) * slots, step), step)
            r.gw[...] += tn(r.mem[span, :], r.dkv[span, :])

        if b == NB - 1:
            for side in range(2):
                r.g[pair_first + side * width : pair_first + (side + 1) * width, :] = half(
                    r.gw[:, side * width : (side + 1) * width]
                )

    def set_sizes(name):
        first, count = layout[name]
        eighth = count // 8
        piece = max(16, eighth // n_line)
        return first, count // 2, eighth, piece, eighth // piece

    def at_rows(start, count):
        return pl.ds(pl.multiple_of(start, 16), count)

    def start(src, dst, at, to):
        pltpu.make_async_remote_copy(
            src_ref=src,
            dst_ref=dst,
            send_sem=r.ssem.at[at],
            recv_sem=r.rsem.at[at],
            device_id=to,
            device_id_type=MESH,
        ).start()

    def wait_rows(ref, count, at, which):
        view = ref.at[pl.ds(0, count), :]
        copy = pltpu.make_async_remote_copy(
            src_ref=view,
            dst_ref=view,
            send_sem=r.ssem.at[at],
            recv_sem=r.rsem.at[at],
            device_id=core_peer,
            device_id_type=MESH,
        )
        copy.wait_recv() if which == "recv" else copy.wait_send()

    def guard(full, cond, body):
        body() if full else pl.when(cond)(body)

    def wait_others(owners, piece, ref, at, which):
        if owners == n_line:
            wait_rows(ref, (n_line - 1) * piece, at, which)
        else:
            if owners > 1:
                pl.when(line < owners)(
                    lambda: wait_rows(ref, (owners - 1) * piece, at, which)
                )
            pl.when(line >= owners)(lambda: wait_rows(ref, owners * piece, at, which))

    def reduce_core(name):
        first, two, eighth, piece, owners = set_sizes(name)
        flights[name, 0] = send(
            r.g.at[at_rows(first + (1 - core) * two, two), :],
            r.rc.at[at_rows(first // 2, two), :],
            set_at[name],
            core_peer,
        )

    def reduce_plane(name):
        first, two, eighth, piece, owners = set_sizes(name)
        flights[name, 0].wait_recv()
        base = first // 2
        for k in (3, 1, 2, 0):
            span = at_rows(base + plane_place(k) * eighth, eighth)
            here = at_rows(first + core * two + plane_place(k) * eighth, eighth)
            r.rc[span, :] = half(wide(r.rc[span, :]) + wide(r.g[here, :]))
            if k:
                flights[name, k] = send(
                    r.rc.at[span, :],
                    r.rp.at[k - 1, pl.ds(first // 8, eighth), :],
                    set_at[name] + k,
                    plane_peer(k),
                )

    def reduce_line(name):
        first, two, eighth, piece, owners = set_sizes(name)
        total = wide(r.rc[at_rows(first // 2 + plane * eighth, eighth), :])
        base = first // 8
        for k in range(1, 4):
            flights[name, k].wait_recv()
            total = total + wide(r.rp[k - 1, base : base + eighth, :])
        r.ps[base : base + eighth, :] = half(total)
        for k in range(1, n_line):

            def go(k=k):
                start(
                    r.ps.at[at_rows(base + line_place(k) * piece, piece), :],
                    r.rz.at[pl.ds((layout_at(name) * n_line + k) * biggest, piece), :],
                    set_at[name] + 4,
                    line_peer(k),
                )

            guard(owners == n_line, line_place(k) < owners, go)

    biggest = max(set_sizes(name)[3] for name in layout)

    def layout_at(name):
        return list(layout).index(name)

    def own_eighth(name):
        first, two, eighth, piece, owners = set_sizes(name)
        return first + core * two + plane * eighth

    def gather_line(name):
        first, two, eighth, piece, owners = set_sizes(name)

        def finish():
            wait_rows(r.rz, (n_line - 1) * piece, set_at[name] + 4, "recv")
            total = wide(r.ps[at_rows(first // 8 + line * piece, piece), :])
            for k in range(1, n_line):
                at = (layout_at(name) * n_line + k) * biggest
                total = total + wide(r.rz[at : at + piece, :])
            here = at_rows(own_eighth(name) + line * piece, piece)
            r.tot[here, :] = half(total)
            for k in range(1, n_line):
                start(r.tot.at[here, :], r.tot.at[here, :], set_at[name] + 5, line_peer(k))

        guard(owners == n_line, line < owners, finish)

    def gather_plane(name):
        first, two, eighth, piece, owners = set_sizes(name)
        wait_others(owners, piece, r.tot, set_at[name] + 5, "recv")
        span = at_rows(own_eighth(name), eighth)
        for k in (3, 1, 2):
            flights[name, 5 + k] = send(
                r.tot.at[span, :], r.tot.at[span, :], set_at[name] + 5 + k, plane_peer(k)
            )

    def gather_core(name):
        first, two, eighth, piece, owners = set_sizes(name)
        for k in range(1, 4):
            flights[name, 5 + k].wait_recv()
        span = at_rows(first + core * two, two)
        flights[name, 9] = send(
            r.tot.at[span, :], r.tot.at[span, :], set_at[name] + 9, core_peer
        )

    def end_set(name):
        first, two, eighth, piece, owners = set_sizes(name)
        flights[name, 9].wait_recv()
        wait_others(owners, piece, r.ps, set_at[name] + 4, "send")
        guard(
            owners == n_line,
            line < owners,
            lambda: wait_rows(r.tot, (n_line - 1) * piece, set_at[name] + 5, "send"),
        )

    def small_core():
        r.v2[pl.ds(core, 1)] = r.vg[...][None]
        flights["v", 0] = send(r.v2.at[core], r.v2.at[core], vec_at, core_peer)

    def small_plane():
        flights["v", 0].wait_recv()
        r.v4[pl.ds(plane, 1)] = (r.v2[0] + r.v2[1])[None]
        for k in (3, 1, 2):
            flights["v", k] = send(
                r.v4.at[plane], r.v4.at[plane], vec_at + k, plane_peer(k)
            )

    def small_line():
        for k in range(1, 4):
            flights["v", k].wait_recv()
        r.vz[pl.ds(line, 1)] = (r.v4[0] + r.v4[1] + r.v4[2] + r.v4[3])[None]
        for k in range(1, n_line):
            start(r.vz.at[line], r.vz.at[line], vec_at + 4, line_peer(k))

    def small_wait(which):
        view = r.vz.at[pl.ds(0, n_line - 1)]
        copy = pltpu.make_async_remote_copy(
            src_ref=view,
            dst_ref=view,
            send_sem=r.ssem.at[vec_at + 4],
            recv_sem=r.rsem.at[vec_at + 4],
            device_id=core_peer,
            device_id_type=MESH,
        )
        copy.wait_recv() if which == "recv" else copy.wait_send()

    def small_end():
        small_wait("recv")
        total = r.vz[0]
        for k in range(1, n_line):
            total = total + r.vz[k]
        r.vtot[...] = total
        small_wait("send")

    def share(i, ref, b):
        at = share_at + 3 * (i * NB + b)
        span = own_span(b, c)
        flights["s", i, b, 0] = send(ref.at[span, :], ref.at[span, :], at, chip_peer)
        flights["s", i, b, 1] = send(ref.at[span, :], ref.at[span, :], at + 1, core_peer)

    def share_on(i, ref, b):
        at = share_at + 3 * (i * NB + b)
        flights["s", i, b, 0].wait_recv()
        span = own_span(b, lax.rem(c + 2, n_cond))
        flights["s", i, b, 2] = send(ref.at[span, :], ref.at[span, :], at + 2, core_peer)

    def share_end():
        for i in range(2):
            for b in range(NB):
                flights["s", i, b, 1].wait_recv()
                flights["s", i, b, 2].wait_recv()

    r.vg[11:16, :] = jnp.zeros((5, width), F32)
    loads["mw"].wait()
    r.mwb[...] = half(r.mw[...])
    loads["mem0"].wait()
    first = list(range(0, part_samples, 2))
    half_way = len(first) // 2
    for s in first[: half_way - 1]:
        pair_forward(s)
    for name in ("act", "vec", "rw"):
        loads[name].wait()
    r.rwb[:, : 4 * width] = half(r.rw[:, : 4 * width])
    pair_forward(first[half_way - 1])
    r.rwb[:, 4 * width :] = half(r.rw[:, 4 * width :])
    loads["mem1"].wait()
    first_forward(0, first[half_way:])
    load_moments()
    loads["mask"].wait()
    loads["flag"].wait()
    usable_rows()
    cross_forward(0)
    pl.semaphore_wait(barrier, len(friends))
    send_mixed(0)
    loads["mem2"].wait()
    loads["mem3"].wait()
    first_forward(1, list(range(part_samples, samples, 2)))
    cross_forward(1)
    send_mixed(1)
    loads["dw"].wait()
    r.dwb[...] = half(r.dw[...])
    loads["cot"].wait()
    middle(0)
    middle(1)
    up_grads()
    reduce_core("up")
    cross_backward(0)
    send_query_grads(0)
    cross_backward_pairs(0)
    reduce_plane("up")
    down_grads()
    reduce_core("down")
    pair_grads(0)
    cross_backward(1)
    send_query_grads(1)
    cross_backward_pairs(1)
    reduce_plane("down")
    pair_grads(1)
    reduce_line("up")
    reduce_core("pair")
    self_backward(0)
    self_backward_rest(0)
    self_backward(1)
    reduce_plane("pair")
    row2_grads()
    row3_grads()
    reduce_core("row2")
    reduce_line("down")
    reduce_plane("row2")
    row1_grads()
    reduce_core("row1")
    gather_line("up")
    reduce_line("pair")
    share(1, r.ga16, 0)
    share(0, r.out16, 1)
    self_backward_rest(1)
    reduce_plane("row1")
    gather_line("down")
    small_core()
    gather_plane("up")
    reduce_line("row2")
    small_plane()
    gather_line("pair")
    reduce_line("row1")
    gather_plane("down")
    share(1, r.ga16, 1)
    gather_line("row2")
    gather_line("row1")
    share_on(1, r.ga16, 0)
    gather_core("up")
    share(0, r.out16, 0)
    small_line()
    share_on(0, r.out16, 1)
    gather_plane("pair")
    gather_plane("row2")
    share_on(1, r.ga16, 1)
    gather_core("down")
    gather_plane("row1")
    gather_core("pair")
    gather_core("row2")
    share_on(0, r.out16, 0)
    gather_core("row1")
    small_end()
    share_end()
    for name in ("m_r", "m_d", "m_p", "a_r", "a_d", "a_p"):
        loads[name].wait()
    for name in layout:
        end_set(name)
    for copy in pending:
        copy.wait_send()


def step_kernel(names, token_count, *refs):
    r = Names()
    for name, ref in zip(names, refs, strict=True):
        setattr(r, name, ref)
    width = r.w_p.shape[0]
    hidden = r.w_d.shape[0]
    keep = 1.0 - (1.0 + STEP) ** (-0.75)
    copies = []

    def store(src, dst):
        copy = pltpu.make_async_copy(src, dst, r.sem.at[len(copies)])
        copy.start()
        copies.append(copy)

    def update(weight, grad, moment, average):
        scaled = grad / token_count
        moment_new = INERTIA * moment + scaled
        weight_new = weight - STEP_RATE * (scaled + INERTIA * moment_new)
        average_new = keep * average + (1.0 - keep) * weight_new
        return moment_new, weight_new, average_new

    def renew(prefix, row, column, first):
        rows = 32
        cols = slice(column, column + width)

        @pl.loop(0, width // rows, unroll=8)
        def _(i):
            at = pl.multiple_of(i * rows, rows)
            grad = wide(r.tot[pl.ds(first + at, rows), :])
            here = pl.ds(row + at, rows)
            old = [getattr(r, kind + "_" + prefix)[here, cols] for kind in "wma"]
            new = update(old[0], grad, old[1], old[2])
            for kind, value in zip("mwa", new):
                getattr(r, prefix + kind)[here, cols] = value

        for kind in "mwa":
            view = (slice(row, row + width), cols)
            store(getattr(r, prefix + kind).at[view], getattr(r, prefix + kind + "_h").at[view])

    pair_first = 2 * hidden + 6 * width
    order = {5: 0, 4: 1, 3: 2, 0: 3, 1: 4, 2: 5}
    blocks = [("d", j * width, 0, hidden + j * width) for j in range(hidden // width)]
    blocks += [("r", 0, (6 + j) * width, j * width) for j in range(hidden // width)]
    blocks += [("r", 0, j * width, 2 * hidden + order[j] * width) for j in range(6)]
    blocks += [("p", 0, j * width, pair_first + j * width) for j in range(2)]

    r.mwb[...] = half(r.w_p[...])
    total_rows = r.dkv.shape[0]
    chunks = 8
    step = total_rows // chunks
    for i in range(chunks):
        for block in blocks[i * len(blocks) // chunks : (i + 1) * len(blocks) // chunks]:
            renew(*block)
        span = pl.ds(i * step, step)
        r.gm[span, :] = nt(r.dkv[span, :], r.mwb[...])
        store(r.gm.at[span, :], r.gm_h.at[span, :])
    r.out[...] = wide(r.out16[...])
    store(r.out, r.out_h)
    r.ga[...] = wide(r.ga16[...])
    store(r.ga, r.ga_h)
    new = update(r.w_v[...], r.vtot[: r.w_v.shape[0], :], r.m_v[...], r.a_v[...])
    for kind, value in zip("mwa", new):
        getattr(r, "v" + kind)[...] = value
        store(getattr(r, "v" + kind), getattr(r, "v" + kind + "_h"))
    for copy in copies:
        copy.wait()


def per_device(
    actions,
    memory,
    patch_flags,
    memory_mask,
    cotangent,
    row_weights,
    memory_weights,
    down_weight,
    vectors,
    row_momentum,
    memory_momentum,
    down_momentum,
    vector_momentum,
    row_average,
    memory_average,
    down_average,
    vector_average,
):
    rows, width = actions.shape
    samples = rows // H
    slots = memory.shape[1]
    hidden = down_weight.shape[0]
    n_cond = lax.axis_size("cond")
    n_dp = lax.axis_size("dp")
    part_rows = rows // NB
    own = part_rows // n_cond
    total = 2 * hidden + 8 * width
    flat = samples * slots
    ins = {
        "act_h": actions,
        "mem_h": memory.reshape(flat, width),
        "mask_h": memory_mask,
        "flag_h": patch_flags.reshape(1, samples),
        "cot_h": cotangent,
        "rw_h": row_weights,
        "mw_h": memory_weights,
        "dw_h": down_weight,
        "vec_h": vectors,
        "m_r_h": row_momentum,
        "m_d_h": down_momentum,
        "m_p_h": memory_momentum,
        "a_r_h": row_average,
        "a_d_h": down_average,
        "a_p_h": memory_average,
    }
    outs = {
        "tot": ((total, width), BF),
        "vtot": ((16, width), F32),
        "dkv": ((flat, 2 * width), BF),
        "out16": ((rows, width), BF),
        "ga16": ((rows, width), BF),
        "rw": (row_weights.shape, F32),
        "dw": (down_weight.shape, F32),
        "mw": (memory_weights.shape, F32),
        "m_r": (row_weights.shape, F32),
        "m_d": (down_weight.shape, F32),
        "m_p": (memory_weights.shape, F32),
        "a_r": (row_weights.shape, F32),
        "a_d": (down_weight.shape, F32),
        "a_p": (memory_weights.shape, F32),
    }

    n_line = n_dp // 2
    biggest = max(16, hidden // 4 // n_line)

    scratch = {
        "act": ((rows, width), F32),
        "vec": (vectors.shape, F32),
        "mem": ((flat, width), BF),
        "mask": (memory_mask.shape, jnp.int32),
        "flag": ((1, samples), jnp.int32),
        "cot": ((rows, width), F32),
        "rwb": (row_weights.shape, BF),
        "mwb": (memory_weights.shape, BF),
        "dwb": (down_weight.shape, BF),
        "blocks": ((256, 256), BF),
        "heads": ((64, 256), F32),
        "heads_b": ((64, 256), BF),
        "a1": ((rows, width), BF),
        "qkv": ((rows, 3 * width), BF),
        "o1": ((rows, width), BF),
        "x1": ((rows, width), F32),
        "a2": ((rows, width), BF),
        "qs": ((rows, width), BF),
        "kv": ((samples, slots, 2 * width), BF),
        "use": ((samples, slots), F32),
        "p": ((samples, 64, slots), BF),
        "ds": ((samples, 64, slots), BF),
        "o_out": ((rows, width), BF),
        "top": ((rows, 128), F32),
        "total": ((rows, 128), F32),
        "st_in": ((NB, n_cond, 16, 128), F32),
        "st_out": ((NB, n_cond, 16, 128), F32),
        "o_in": ((NB, n_cond, own, width), BF),
        "o2": ((NB * own, width), BF),
        "a3": ((NB * own, width), BF),
        "dz": ((NB * own, width), BF),
        "hb": ((NB * own, hidden), BF),
        "du": ((NB * own, hidden), BF),
        "dx2": ((NB * own, width), F32),
        "dx1": ((NB * own, width), F32),
        "dy2": ((NB * own, width), BF),
        "dqc": ((NB * own, width), BF),
        "dy1": ((NB * own, width), BF),
        "dqkv": ((NB * own, 3 * width), BF),
        "do_in": ((rows, width), BF),
        "do_out": ((NB, n_cond, own, width), BF),
        "dl_in": ((NB, n_cond, 8, 128), F32),
        "dl_out": ((NB, n_cond, 8, 128), F32),
        "dl": ((rows, 128), F32),
        "dq_out": ((rows, width), BF),
        "dq_in": ((NB, n_cond, own, width), BF),
        "vg": ((16, width), F32),
        "v2": ((2, 16, width), F32),
        "v4": ((4, 16, width), F32),
        "vz": ((n_line, 16, width), F32),
        "g": ((total, width), BF),
        "gw": ((width, 2 * width), F32),
        "rc": ((total // 2, width), BF),
        "rp": ((3, total // 8, width), BF),
        "ps": ((total // 8, width), BF),
        "rz": ((6 * n_line * biggest, width), BF),
    }
    sems = {
        "load_sem": pltpu.SemaphoreType.DMA((24,)),
        "ssem": pltpu.SemaphoreType.DMA((128,)),
        "rsem": pltpu.SemaphoreType.DMA((128,)),
    }
    whole = pl.BlockSpec(memory_space=pltpu.VMEM)
    far = pl.BlockSpec(memory_space=pltpu.HBM)
    names = list(ins) + list(outs) + list(scratch) + list(sems)
    sizes = (rows, samples, slots, n_cond, n_dp, width)
    made = pl.pallas_call(
        functools.partial(layer_kernel, names, sizes),
        out_shape=[pltpu.VMEM(*v) for v in outs.values()],
        in_specs=[far] * len(ins),
        out_specs=[whole] * len(outs),
        scratch_shapes=[pltpu.VMEM(*v) for v in scratch.values()] + list(sems.values()),
        compiler_params=pltpu.CompilerParams(
            collective_id=0, has_side_effects=True, vmem_limit_bytes=32 * MIB
        ),
        name="layer",
    )(*(pltpu.with_memory_space_constraint(v, pltpu.HBM) for v in ins.values()))

    ins2 = dict(zip(outs, made, strict=True))
    ins2 |= {"w_v": vectors, "m_v": vector_momentum, "a_v": vector_average}
    outs2 = {
        "out": (rows, width),
        "ga": (rows, width),
        "gm": (flat, width),
    }
    for prefix, array in (("r", row_weights), ("p", memory_weights), ("d", down_weight), ("v", vectors)):
        for kind in "mwa":
            outs2[prefix + kind] = array.shape
    renamed = {"rw": "w_r", "dw": "w_d", "mw": "w_p"}
    names2 = [renamed.get(k, k) for k in ins2]
    names2 += [k + "_h" for k in outs2] + list(outs2) + ["mwb", "sem"]
    results = pl.pallas_call(
        functools.partial(step_kernel, names2, float(rows * n_dp)),
        out_shape=[jax.ShapeDtypeStruct(v, F32) for v in outs2.values()],
        in_specs=[whole] * len(ins2),
        out_specs=[far] * len(outs2),
        scratch_shapes=[pltpu.VMEM(v, F32) for v in outs2.values()]
        + [pltpu.VMEM(memory_weights.shape, BF), pltpu.SemaphoreType.DMA((64,))],
        compiler_params=pltpu.CompilerParams(vmem_limit_bytes=26 * MIB),
        name="step",
    )(*ins2.values())
    out, ga, gm = results[:3]
    return (out, ga, gm.reshape(samples, slots, width), *results[3:])


def solution(mesh):
    in_specs = (
        P("dp", None),
        P("dp", "cond", None),
        P("dp", "cond"),
        P("dp", "cond"),
        P("dp", None),
    ) + (P(),) * 12
    out_specs = (P("dp", None), P("dp", None), P("dp", "cond", None)) + (P(),) * 12
    return jax.shard_map(
        per_device, mesh=mesh, in_specs=in_specs, out_specs=out_specs, check_vma=False
    )
```
